32 devices in a mesh: row: 4 (over z), col: 8 (over y, x, core).
Axes of the slice: x: 2, y: 2, z: 4, core: 2. Of those that a mesh axis runs over, the one named last changes fastest.
Arguments:
- a_blocks: float32 [256, 8, 256, 256], P(('row', 'col')), may hold values from -0.09375 to 0.09375
- a_live: int32 [256, 8], P(('row', 'col')), may hold values from 0 to 1, as said below
- p_blocks: float32 [256, 256, 2, 128], P(('row', 'col')), may hold values from -0.1875 to 0.1875
- p_cols: int32 [256, 2], P(('row', 'col')), may hold values from 0 to 31, as said below
- ghost_list: int32 [256, 7], P(('row', 'col')), may hold values from 0 to 7, as said below
- policy: int32 [256], P(('row', 'col')), may hold values from 0 to 15
- rates: float32 [16, 256], replicated, may hold values from 0.1 to 1
- rhs: float32 [4096, 256], P(('row', 'col')), may hold values from -6 to 6
- guess: float32 [4096, 256], P(('row', 'col')), may hold values from -6 to 6
Outputs:
- coarse: float32 [4096, 4, 8, 128], P('row', None, 'col')
- smoothed: float32 [4096, 256], P(('row', 'col'))
The draws below stay inside these ranges and needn't reach their ends.
Inputs may be any that keep to these rules, and one draw needn't show every extreme that they name: a_live[i, 0] is 1 for every i. On each device and for each k, the entries ghost_list[d * 8 + s, k] over s = 0 .. 7 are a permutation of 0 .. 7. p_cols[j, m] modulo the number of col devices equals (col index of the device holding block row j + m * 8) modulo that number. The quotient by that number names a mesh row: among the 16 entries of one device at most 4 name the same mesh row, and the device's own mesh row is named exactly 4 times, by at least one entry of each m.
All inputs are finite; a program needn't handle non-finite values.
Results may differ from the reference program's by a relative error of at most 0.0003.
Values sent between devices are 32-bit elements; how exact they have to be, the bound alone decides.
A program may use at most 192 MiB of HBM per device.

```python
import math
import jax
import jax.numpy as jnp
from jax import lax

BS = 256
CB = 128
KA = 8
KP = 2
NPOL = 16
NCOL = 256
NB = 8
NFB = 256
NC = 4096
RCAP = 4
N_ROW = 4
N_COL = 8
DEVICES = 32


def pattern(key):
    base = jax.random.fold_in(key, 1301)
    key_perm, key_pad, key_pick, key_score, key_rest = jax.random.split(base, 5)
    device = jnp.arange(DEVICES, dtype=jnp.int32)
    row_of = device // N_COL
    col_of = device % N_COL
    within = jnp.arange(NB, dtype=jnp.int32)
    perm_keys = jax.random.randint(key_perm, (DEVICES, KA - 1, NB), 0, 1 << 20) * NB + within
    orders = jnp.argsort(perm_keys, axis=-1).astype(jnp.int32)
    ghost = orders.transpose(0, 2, 1).reshape(NFB, KA - 1)
    padding = jax.random.randint(key_pad, (NFB, KA - 1), 0, 8)
    live = jnp.concatenate([jnp.ones((NFB, 1), jnp.int32), (padding != 0).astype(jnp.int32)], axis=1)
    pair_count = NB * KP
    pair = jnp.arange(pair_count, dtype=jnp.int32)
    pair_m = pair % KP
    pair_t = pair // KP
    first_t = jax.random.randint(key_pick, (DEVICES, KP), 0, NB)
    chosen = pair_t[None, :] == first_t[:, pair_m]
    score = jax.random.randint(key_score, (DEVICES, pair_count), 0, 1 << 20) * pair_count + pair
    score = jnp.where(chosen, -1 - pair[None, :], score)
    ranks = jnp.argsort(jnp.argsort(score, axis=1), axis=1).astype(jnp.int32)
    forced = ranks < RCAP
    pool_size = (N_ROW - 1) * RCAP
    places = jnp.arange(pool_size, dtype=jnp.int32)
    pool_vals = (row_of[:, None] + 1 + places[None, :] // RCAP) % N_ROW
    pool_keys = jax.random.randint(key_rest, (DEVICES, pool_size), 0, 1 << 20) * pool_size + places
    shuffled = jnp.take_along_axis(pool_vals, jnp.argsort(pool_keys, axis=1), axis=1)
    others = jnp.take_along_axis(shuffled, jnp.clip(ranks - RCAP, 0, pool_size - 1), axis=1)
    groups = jnp.where(forced, row_of[:, None], others)
    coarse_cols = N_COL * groups + (col_of[:, None] + pair_m[None, :] * KA) % N_COL
    return (live, coarse_cols.reshape(NFB, KP).astype(jnp.int32), ghost)


def draw_a_live(key, part):
    return pattern(key)[0]


def draw_p_cols(key, part):
    return pattern(key)[1]


def draw_ghost_list(key, part):
    return pattern(key)[2]


def place_ends(drawn, key, smallest, high):
    dims = drawn.shape
    place = [jax.random.randint(jax.random.fold_in(key, axis), (), 0, dims[axis]) for axis in range(len(dims))]
    drawn = drawn.at[tuple(place)].set(smallest)
    longest = dims.index(max(dims))
    place[longest] = (place[longest] + 1) % dims[longest]
    return drawn.at[tuple(place)].set(high)


def levels(key, shape, cuts, least, top_value):
    factor_of = 1.0
    for axis_at, blocks in cuts:
        heights = jax.random.uniform(jax.random.fold_in(jax.random.fold_in(key, 6), axis_at), (blocks,), jnp.float32, least / len(cuts), top_value / len(cuts))
        factor_of = factor_of * jnp.repeat(jnp.exp(heights), shape[axis_at] // blocks).reshape((-1,) + (1,) * (len(shape) - 1 - axis_at))
    return factor_of


def noise(own_key, extent, deviation, most, cuts=(), held_as=jnp.bfloat16):
    loudness = levels(own_key, extent, cuts, -0.22, 0.18) if cuts else 1.0
    drawn = jax.random.normal(own_key, extent, jnp.float32) * deviation * loudness
    return jnp.minimum(jnp.maximum(drawn, -most), most).astype(held_as)


def setup_inputs(seed: int = 0) -> dict:
    key_of = jax.random.split(jax.random.key(seed), 10)
    a_blocks = noise(key_of[0], (NFB, KA, BS, BS), 0.015625, 0.09375, ((0, 32),), jnp.float32)
    a_live = draw_a_live(jax.random.fold_in(key_of[9], 71), 0)
    p_blocks = noise(key_of[2], (NFB, BS, KP, CB), (4 * BS) ** -0.5, 0.1875, ((0, 32),), jnp.float32)
    p_cols = draw_p_cols(jax.random.fold_in(key_of[9], 71), 0)
    ghost_list = draw_ghost_list(jax.random.fold_in(key_of[9], 71), 0)
    policy = place_ends(jax.random.randint(key_of[5], (NFB,), 0, NPOL), jax.random.fold_in(key_of[5], 1), 0, NPOL - 1).astype(jnp.int32)
    rates = jnp.clip(jnp.exp(jax.random.uniform(key_of[6], (NPOL, BS), jnp.float32, math.log(0.1), math.log(1.0))), 0.1, 1.0)
    rhs = noise(key_of[7], (NC, NCOL), 1.0, 6.0, ((0, 32),), jnp.float32)
    guess = noise(key_of[8], (NC, NCOL), 1.0, 6.0, ((0, 32),), jnp.float32)
    return {"a_blocks": a_blocks, "a_live": a_live, "p_blocks": p_blocks, "p_cols": p_cols, "ghost_list": ghost_list, "policy": policy, "rates": rates, "rhs": rhs, "guess": guess}


damping = 0.7


def reference(a_blocks, a_live, p_blocks, p_cols, ghost_list, policy, rates, rhs, guess):
    highest = lax.Precision.HIGHEST
    prolong = p_blocks.reshape(NFB, BS, KP * CB)
    later = jnp.arange(1, KA, dtype=jnp.int32)

    def one_row(coarse, index):
        device = index // NB
        within = index % NB
        source = (device // N_COL) * N_COL + (device % N_COL - later) % N_COL
        picks = source * NB + ghost_list[source * NB + within, later - 1]
        block_cols = jnp.concatenate([index[None], picks]).astype(jnp.int32)
        ghost = prolong[block_cols]
        ghost_cols = p_cols[block_cols]
        blocks = a_blocks[index] * a_live[index][:, None, None].astype(a_blocks.dtype)
        blocks = blocks.at[0].add(jnp.diag(rates[policy[index]]))
        product = jnp.einsum('kab,kbn->kan', blocks, ghost, precision=highest)
        partial_value = jnp.einsum('am,kan->kmn', prolong[index], product, precision=highest)
        partial_value = partial_value.reshape(KA, KP, CB, KP, CB).transpose(0, 1, 3, 2, 4)
        row_sel = jnp.broadcast_to(p_cols[index][None, :, None], (KA, KP, KP))
        col_sel = jnp.broadcast_to(ghost_cols[:, None, :], (KA, KP, KP))
        return coarse.at[row_sel, col_sel].add(partial_value), None

    start_blocks = jnp.zeros((DEVICES, DEVICES, CB, CB), jnp.float32)
    coarse, _ = lax.scan(one_row, start_blocks, jnp.arange(NFB, dtype=jnp.int32))
    matrix = coarse.transpose(0, 2, 1, 3).reshape(NC, NC)
    floor_diag = jnp.maximum(jnp.abs(jnp.diagonal(matrix)), 1.0)
    current = guess
    for sweep in range(2):
        applied = jnp.dot(matrix, current, precision=highest)
        current = current + damping * (rhs - applied) / floor_diag[:, None]
    return matrix.reshape(NC, N_ROW, N_COL, CB), current
```

```python
import functools

import jax
import jax.numpy as jnp
from jax import lax
from jax.experimental import pallas as pl
from jax.experimental.pallas import tpu as pltpu
from jax.sharding import PartitionSpec as P

BS = 256
CB = 128
KA = 8
KP = 2
NPOL = 16


damping = 0.7


def from_behind(value, axis, steps):
    count = lax.axis_size(axis)
    pairs = [(source, (source + steps) % count) for source in range(count)]
    return lax.ppermute(value, axis, pairs)


def any_mesh(a_blocks, a_live, p_blocks, p_cols, ghost_list, policy, rates, rhs, guess):
    highest = lax.Precision.HIGHEST
    row_count = lax.axis_size("row")
    col_count = lax.axis_size("col")
    dev_count = row_count * col_count
    row_here = lax.axis_index("row")
    col_here = lax.axis_index("col")
    local_rows = a_blocks.shape[0]
    own_p = p_blocks.reshape(local_rows, BS, KP * CB)
    send_p = []
    send_c = []
    for offset in range(1, KA):
        picks = ghost_list[:, offset - 1]
        send_p.append(own_p[picks])
        send_c.append(p_cols[picks].astype(jnp.float32))
    incoming_p = [own_p]
    incoming_c = [p_cols]
    for offset in range(1, KA):
        moved_p, moved_c = from_behind((send_p[offset - 1], send_c[offset - 1]), "col", offset)
        incoming_p.append(moved_p)
        incoming_c.append(moved_c.astype(jnp.int32))
    ghost_p = jnp.stack(incoming_p, axis=1)
    ghost_c = jnp.stack(incoming_c, axis=1)
    live = a_live.astype(jnp.float32)
    selector = (policy[:, None] == jnp.arange(NPOL, dtype=jnp.int32)[None, :]).astype(jnp.float32)
    rate_rows = jnp.dot(selector, rates, precision=highest)
    product = jnp.einsum("skab,skbn->skan", a_blocks, ghost_p, precision=highest)
    product = product * live[:, :, None, None]
    product = product.at[:, 0].add(rate_rows[:, :, None] * own_p)
    partial_value = jnp.einsum("sam,skan->skmn", own_p, product, precision=highest)
    partial_value = (
        partial_value.reshape(local_rows, KA, KP, CB, KP, CB)
        .transpose(0, 1, 2, 4, 3, 5)
        .reshape(-1, CB, CB)
    )
    first = jnp.broadcast_to(p_cols[:, None, :, None], (local_rows, KA, KP, KP)).reshape(-1)
    second = jnp.broadcast_to(ghost_c[:, :, None, :], (local_rows, KA, KP, KP)).reshape(-1)
    alive = jnp.broadcast_to(a_live[:, :, None, None] > 0, (local_rows, KA, KP, KP)).reshape(-1)
    owner = first // col_count * col_count + second % col_count
    spot = first % col_count * row_count + second // col_count
    order = jnp.arange(owner.shape[0], dtype=jnp.int32)
    earlier = (
        (owner[None, :] == owner[:, None]) & alive[None, :] & (order[None, :] < order[:, None])
    )
    rank = jnp.sum(earlier.astype(jnp.int32), axis=1)
    row_cap = max(2, -(-(local_rows * KP) // row_count))
    slot_cap = row_cap * max(1, KA * KP // col_count)
    slot = jnp.where(alive, owner * slot_cap + rank, dev_count * slot_cap)
    sent_blocks = jax.ops.segment_sum(partial_value, slot, num_segments=dev_count * slot_cap + 1)[
        :-1
    ]
    sent_spots = jax.ops.segment_sum(
        (spot + 1).astype(jnp.float32), slot, num_segments=dev_count * slot_cap + 1
    )[:-1]
    got_blocks, got_spots = (
        lax.all_to_all(
            sent_blocks.reshape(dev_count, slot_cap, CB, CB),
            ("row", "col"),
            split_axis=0,
            concat_axis=0,
            tiled=True,
        ),
        lax.all_to_all(
            sent_spots.reshape(dev_count, slot_cap),
            ("row", "col"),
            split_axis=0,
            concat_axis=0,
            tiled=True,
        ),
    )
    places = got_spots.reshape(-1).astype(jnp.int32) - 1
    places = jnp.where(places < 0, dev_count, places)
    summed = jax.ops.segment_sum(
        got_blocks.reshape(-1, CB, CB), places, num_segments=dev_count + 1
    )[:-1]
    coarse = (
        summed.reshape(col_count, row_count, CB, CB)
        .transpose(0, 2, 1, 3)
        .reshape(col_count * CB, row_count, 1, CB)
    )
    matrix = coarse.reshape(col_count * CB, row_count * CB)
    own_block = lax.dynamic_slice(matrix, (col_here * CB, row_here * CB), (CB, CB))
    floor_diag = jnp.maximum(jnp.abs(jnp.diagonal(own_block)), 1.0)
    current = guess
    for sweep in range(2):
        gathered = lax.all_gather(current, "row", axis=0, tiled=True)
        applied = lax.psum_scatter(
            jnp.dot(matrix, gathered, precision=highest), "col", scatter_dimension=0, tiled=True
        )
        current = current + damping * (rhs - applied) / floor_diag[:, None]
    return (coarse, current)


MESH = pl.DeviceIdType.MESH
QUOT = KA


def halves(value):
    high = value.astype(jnp.bfloat16)
    return high, (value - high.astype(jnp.float32)).astype(jnp.bfloat16)


def beside(value):
    high, low = halves(value)
    return jnp.concatenate([high, high, low], axis=1)


def below(value):
    high, low = halves(value)
    return jnp.concatenate([high, low, high], axis=0)


def dot(left, right):
    return jnp.dot(left, right, preferred_element_type=jnp.float32)


def spread(value, names, count):
    parts = []
    for group in range(count):
        part = 0.0
        for m, name in enumerate(names):
            part = part + jnp.where(name == group, value[:, m * CB : (m + 1) * CB], 0.0)
        parts.append(part)
    return jnp.concatenate(parts, axis=1)


def kernel(
    rows, cols, a_ref, p_ref, meta_ref, own_ref, live_ref, rate_ref, rhs_ref, guess_ref,
    matrix, out_ref,
    pall, part, got, ecat, abuf0, abuf1, metas, meta_s, x_all, r_out, r_in,
    a_sem, l_sem, p_send, p_recv, m_send, m_recv, z_send, z_recv, s_send, s_recv,
    x_send, x_recv, r_send, r_recv,
):
    q = lax.axis_index("row")
    c = lax.axis_index("col")
    last = rows - 1
    blocks = pall.shape[1]
    digit_y, digit_x, core = c // 4, (c // 2) % 2, c % 2
    other = 1 - core
    swap_y, swap_x, swap_c = 1 - 2 * digit_y, 1 - 2 * digit_x, 1 - 2 * core

    def peer(flips):
        return c + flips[0] * swap_y * 4 + flips[1] * swap_x * 2 + flips[2] * swap_c

    to_flips = [
        (0, 0, 0), (0, 0, 1), (core, other, 0), (other, core, 1),
        (other, core, 0), (core, other, 1), (1, 1, 0), (1, 1, 1),
    ]
    from_flips = list(to_flips)
    from_flips[3], from_flips[5] = to_flips[5], to_flips[3]
    target = [peer(flips) for flips in to_flips]
    origin = [peer(flips) for flips in from_flips]
    plain = [peer((f // 4, (f // 2) % 2, f % 2)) for f in range(cols)]
    slot_k = [lax.rem(c - e + cols, cols) for e in target]
    abufs = [abuf0, abuf1]

    def remote(src, dst, send, recv, row, col):
        return pltpu.make_async_remote_copy(
            src_ref=src, dst_ref=dst, send_sem=send, recv_sem=recv,
            device_id=(row, col), device_id_type=MESH,
        )

    def load_a(t):
        return pltpu.make_async_copy(
            a_ref.at[:, slot_k[t]], abufs[t % 2], a_sem.at[t % 2]
        )

    own_p = pltpu.make_async_copy(p_ref, pall.at[0], l_sem.at[0])
    own_p.start()
    load_a(0).start()
    own_meta = pltpu.make_async_copy(meta_ref, metas.at[c], l_sem.at[1])
    own_meta.start()
    own_x = pltpu.make_async_copy(guess_ref, x_all.at[0, q], l_sem.at[2])
    own_x.start()

    barrier = pltpu.get_barrier_semaphore()
    for f in range(1, cols):
        pl.semaphore_signal(barrier, inc=1, device_id=(q, plain[f]), device_id_type=MESH)
    row_peer = [lax.rem(q + step, rows) for step in range(rows)]
    for step in range(1, rows):
        pl.semaphore_signal(barrier, inc=1, device_id=(row_peer[step], c), device_id_type=MESH)
    pl.semaphore_wait(barrier, cols - 1 + rows - 1)

    mid = blocks // 2
    p_copies = [
        remote(p_ref, pall.at[1], p_send.at[0], p_recv.at[0], q, target[1]),
        remote(p_ref, pall.at[2], p_send.at[1], p_recv.at[1], q, target[2]),
        remote(p_ref, pall.at[4], p_send.at[2], p_recv.at[2], q, target[4]),
        remote(pall.at[2], pall.at[3], p_send.at[3], p_recv.at[3], q, target[1]),
        remote(pall.at[4], pall.at[5], p_send.at[4], p_recv.at[4], q, target[1]),
        remote(
            pall.at[4, pl.ds(0, mid)], pall.at[6, pl.ds(0, mid)],
            p_send.at[5], p_recv.at[5], q, target[2],
        ),
        remote(
            pall.at[2, pl.ds(mid, blocks - mid)], pall.at[6, pl.ds(mid, blocks - mid)],
            p_send.at[6], p_recv.at[6], q, target[4],
        ),
        remote(pall.at[6], pall.at[7], p_send.at[7], p_recv.at[7], q, target[1]),
    ]
    m_copies = [
        remote(meta_ref, metas.at[c], m_send.at[f], m_recv.at[f], q, plain[f])
        for f in range(1, cols)
    ]

    p_copies[0].start()
    p_copies[1].start()
    for copy in m_copies:
        copy.start()

    def x_copies(sweep):
        return [
            remote(
                x_all.at[sweep, q], x_all.at[sweep, q],
                x_send.at[sweep, step], x_recv.at[sweep, step], row_peer[step], c,
            )
            for step in range(1, rows)
        ]

    own_p.wait()

    def widen(s, _):
        names = [own_ref[s, m] for m in range(KP)]
        ecat[s] = beside(spread(pall[0, s], names, rows).T)
        return 0

    lax.fori_loop(0, blocks, widen, 0)

    eye = lax.broadcasted_iota(jnp.int32, (BS, BS), 0) == lax.broadcasted_iota(
        jnp.int32, (BS, BS), 1
    )

    def compute(t):
        load_a(t).wait()
        if t + 1 < KA:
            load_a(t + 1).start()
        abuf = abufs[t % 2]

        def one(j, _):
            if t == 0:
                s = j
                names = [own_ref[j, m] for m in range(KP)]
            else:
                s = meta_s[target[t], j, slot_k[t] - 1]
                names = [meta_s[target[t], j, QUOT + m] for m in range(KP)]
            block = abuf[s] * live_ref[s, slot_k[t]].astype(jnp.float32)
            if t == 0:
                block = block + jnp.where(eye, rate_ref[pl.ds(j, 1), :], 0.0)
            product = dot(beside(block), below(pall[t, j]))
            wide = below(spread(product, names, rows))
            for group in range(rows):
                more = dot(ecat[s, group * CB : (group + 1) * CB, :], wide)
                part[t, group] = jnp.where(j == 0, 0.0, part[t, group]) + more
            return 0

        lax.fori_loop(0, blocks, one, 0)

    def z_copy(t, up, away, source):
        group = q + away if up else q - away
        to_row = q + 1 if up else q - 1
        slot = rows if (not up and away == 1) else group
        return remote(
            source.at[t, group], got.at[t, slot],
            z_send.at[t, int(up), away], z_recv.at[t, slot], to_row, c,
        )

    def z_got(t, slot):
        return remote(
            got.at[t, slot], got.at[t, slot],
            z_send.at[t, 0, 0], z_recv.at[t, slot], q, c,
        )

    def z_start(t):
        for away in range(last, 0, -1):
            for up in (True, False):
                @pl.when(q == (0 if up else last))
                def _():
                    z_copy(t, up, away, part).start()

    def z_pass(t):
        for away in range(last - 1, 0, -1):
            for up in (True, False):
                inside = (q > 0) & (q + away <= last) if up else (q < last) & (q - away >= 0)

                @pl.when(inside)
                def _():
                    group = q + away if up else q - away
                    z_got(t, group).wait_recv()
                    got[t, group] = got[t, group] + part[t, group]
                    z_copy(t, up, away, got).start()

    def z_wait(t):
        for away in range(1, rows):
            for up in (True, False):
                there = (q + away <= last) if up else (q - away >= 0)

                @pl.when(there)
                def _():
                    z_copy(t, up, away, part).wait_send()

    def strip_copy(t):
        return remote(
            part.at[t, q], matrix.at[c], s_send.at[t], s_recv.at[t], q, target[t]
        )

    def finish(t):
        @pl.when(q > 0)
        def _():
            z_got(t, q).wait_recv()
            part[t, q] = part[t, q] + got[t, q]

        @pl.when(q < last)
        def _():
            z_got(t, rows).wait_recv()
            part[t, q] = part[t, q] + got[t, rows]

        if t == 0:
            matrix[c] = part[0, q]
        else:
            strip_copy(t).start()

    for t in range(KA):
        if t == 1:
            own_meta.wait()
            for copy in m_copies:
                copy.wait_recv()
            to_smem = pltpu.make_async_copy(metas, meta_s, l_sem.at[3])
            to_smem.start()
            to_smem.wait()
            p_copies[0].wait_recv()
        if t == 2:
            p_copies[1].wait_recv()
            p_copies[3].start()
            p_copies[1].wait_send()
            p_copies[2].start()
        if t == 3:
            p_copies[3].wait_recv()
        if t == 4:
            p_copies[2].wait_recv()
            p_copies[4].start()
            p_copies[2].wait_send()
            p_copies[5].start()
            p_copies[6].start()
        if t == 5:
            p_copies[4].wait_recv()
        if t == 6:
            p_copies[5].wait_recv()
            p_copies[6].wait_recv()
            p_copies[7].start()
        if t == 7:
            p_copies[7].wait_recv()
        compute(t)
        z_start(t)
        if t == 1:
            own_x.wait()
            for copy in x_copies(0):
                copy.start()
        if t >= 1:
            z_pass(t - 1)
        if t >= 2:
            finish(t - 2)
    z_pass(KA - 1)
    finish(KA - 2)
    finish(KA - 1)

    def r_copy(sweep, t):
        return remote(
            r_out.at[sweep, t], r_in.at[sweep, t],
            r_send.at[sweep, t], r_recv.at[sweep, t], q, origin[t],
        )

    same = lax.broadcasted_iota(jnp.int32, (CB, CB), 0) == lax.broadcasted_iota(
        jnp.int32, (CB, CB), 1
    )
    diagonal = jnp.zeros((CB, 1), jnp.float32)
    for group in range(rows):
        block = matrix[c, :, group * CB : (group + 1) * CB]
        kept = jnp.where(same & (q == group), block, 0.0)
        diagonal = diagonal + jnp.sum(kept, axis=1, keepdims=True)
    scale = damping / jnp.maximum(jnp.abs(diagonal), 1.0)

    current = guess_ref[...]
    for sweep in range(2):
        if sweep == 1:
            x_all[1, q] = current
            for copy in x_copies(1):
                copy.start()
        for copy in x_copies(sweep):
            copy.wait_recv()
        x_wide = below(x_all[sweep].reshape(rows * CB, x_all.shape[3]))
        for t in range(KA - 1, -1, -1) if sweep else range(KA):
            if sweep == 0 and t > 0:
                strip_copy(t).wait_recv()
            r_out[sweep, t] = dot(beside(matrix[origin[t]]), x_wide)
            if t > 0:
                r_copy(sweep, t).start()
        applied = r_out[sweep, 0]
        for t in range(1, KA):
            r_copy(sweep, t).wait_recv()
            applied = applied + r_in[sweep, t]
        current = current + scale * (rhs_ref[...] - applied)
    out_ref[...] = current

    for copy in p_copies + m_copies + x_copies(0) + x_copies(1):
        if copy is not p_copies[1] and copy is not p_copies[2]:
            copy.wait_send()
    for t in range(KA):
        z_wait(t)
        if t > 0:
            strip_copy(t).wait_send()
            r_copy(0, t).wait_send()
            r_copy(1, t).wait_send()


def col_mesh(a_blocks, a_live, p_blocks, p_cols, ghost_list, policy, rates, rhs, guess):
    rows = lax.axis_size("row")
    cols = lax.axis_size("col")
    blocks = a_blocks.shape[0]
    width = rhs.shape[1]
    own_p = p_blocks.reshape(blocks, BS, KP * CB)
    selector = (policy[:, None] == jnp.arange(NPOL, dtype=jnp.int32)[None, :]).astype(jnp.float32)
    rate_rows = jnp.dot(selector, rates, precision=lax.Precision.HIGHEST)
    order = jnp.arange(blocks, dtype=jnp.int32)
    held_at = jnp.sum(
        jnp.where(ghost_list[:, None, :] == order[None, :, None], order[:, None, None], 0), axis=0
    )
    names = p_cols // cols
    meta = jnp.concatenate(
        [
            jnp.pad(held_at, ((0, 0), (0, QUOT - held_at.shape[1]))),
            jnp.pad(names, ((0, 0), (0, CB - QUOT - KP))),
        ],
        axis=1,
    )
    vmem = pl.BlockSpec(memory_space=pltpu.VMEM)
    smem = pl.BlockSpec(memory_space=pltpu.SMEM)
    anywhere = pl.BlockSpec(memory_space=pl.ANY)
    f32, bf16 = jnp.float32, jnp.bfloat16
    dma = pltpu.SemaphoreType.DMA
    matrix, smoothed = pl.pallas_call(
        functools.partial(kernel, rows, cols),
        out_shape=(
            jax.ShapeDtypeStruct((cols, CB, rows * CB), f32),
            jax.ShapeDtypeStruct((CB, width), f32),
        ),
        in_specs=[anywhere, anywhere, vmem, smem, smem, vmem, vmem, vmem],
        out_specs=(vmem, vmem),
        scratch_shapes=[
            pltpu.VMEM((KA, blocks, BS, KP * CB), f32),
            pltpu.VMEM((KA, rows, CB, rows * CB), f32),
            pltpu.VMEM((KA, rows + 1, CB, rows * CB), f32),
            pltpu.VMEM((blocks, rows * CB, 3 * BS), bf16),
            pltpu.VMEM((blocks, BS, BS), f32),
            pltpu.VMEM((blocks, BS, BS), f32),
            pltpu.VMEM((cols, blocks, CB), jnp.int32),
            pltpu.SMEM((cols, blocks, CB), jnp.int32),
            pltpu.VMEM((2, rows, CB, width), f32),
            pltpu.VMEM((2, KA, CB, width), f32),
            pltpu.VMEM((2, KA, CB, width), f32),
            dma((2,)), dma((4,)), dma((8,)), dma((8,)), dma((cols,)), dma((cols,)),
            dma((KA, 2, rows)), dma((KA, rows + 1)), dma((KA,)), dma((KA,)),
            dma((2, rows)), dma((2, rows)), dma((2, KA)), dma((2, KA)),
        ],
        compiler_params=pltpu.CompilerParams(
            collective_id=0, has_side_effects=True, vmem_limit_bytes=60 * 1024 * 1024
        ),
        cost_estimate=pl.CostEstimate(
            flops=6 * KA * blocks * BS * BS * (BS + rows * CB),
            bytes_accessed=4 * (a_blocks.size + p_blocks.size), transcendentals=0,
        ),
        name="coarse_and_sweeps",
    )(a_blocks, own_p, meta, names, a_live, rate_rows, rhs, guess)
    return matrix.reshape(cols * CB, rows, 1, CB), smoothed


def on_device(a_blocks, *rest):
    if lax.axis_size("col") == a_blocks.shape[1]:
        return col_mesh(a_blocks, *rest)
    return any_mesh(a_blocks, *rest)


def solution(mesh):
    return jax.shard_map(
        on_device,
        mesh=mesh,
        in_specs=(
            P(("row", "col"), None, None, None),
            P(("row", "col"), None),
            P(("row", "col"), None, None, None),
            P(("row", "col"), None),
            P(("row", "col"), None),
            P(("row", "col")),
            P(),
            P(("row", "col"), None),
            P(("row", "col"), None),
        ),
        out_specs=(P("row", None, "col", None), P(("row", "col"), None)),
        check_vma=False,
    )
```

```python
import functools

import jax
import jax.numpy as jnp
from jax import lax
from jax.experimental import pallas as pl
from jax.experimental.pallas import tpu as pltpu
from jax.sharding import PartitionSpec as P

BS = 256
CB = 128
KA = 8
KP = 2
NPOL = 16


damping = 0.7


def from_behind(value, axis, steps):
    count = lax.axis_size(axis)
    pairs = [(source, (source + steps) % count) for source in range(count)]
    return lax.ppermute(value, axis, pairs)


def any_mesh(a_blocks, a_live, p_blocks, p_cols, ghost_list, policy, rates, rhs, guess):
    highest = lax.Precision.HIGHEST
    row_count = lax.axis_size("row")
    col_count = lax.axis_size("col")
    dev_count = row_count * col_count
    row_here = lax.axis_index("row")
    col_here = lax.axis_index("col")
    local_rows = a_blocks.shape[0]
    own_p = p_blocks.reshape(local_rows, BS, KP * CB)
    send_p = []
    send_c = []
    for offset in range(1, KA):
        picks = ghost_list[:, offset - 1]
        send_p.append(own_p[picks])
        send_c.append(p_cols[picks].astype(jnp.float32))
    incoming_p = [own_p]
    incoming_c = [p_cols]
    for offset in range(1, KA):
        moved_p, moved_c = from_behind((send_p[offset - 1], send_c[offset - 1]), "col", offset)
        incoming_p.append(moved_p)
        incoming_c.append(moved_c.astype(jnp.int32))
    ghost_p = jnp.stack(incoming_p, axis=1)
    ghost_c = jnp.stack(incoming_c, axis=1)
    live = a_live.astype(jnp.float32)
    selector = (policy[:, None] == jnp.arange(NPOL, dtype=jnp.int32)[None, :]).astype(jnp.float32)
    rate_rows = jnp.dot(selector, rates, precision=highest)
    product = jnp.einsum("skab,skbn->skan", a_blocks, ghost_p, precision=highest)
    product = product * live[:, :, None, None]
    product = product.at[:, 0].add(rate_rows[:, :, None] * own_p)
    partial_value = jnp.einsum("sam,skan->skmn", own_p, product, precision=highest)
    partial_value = (
        partial_value.reshape(local_rows, KA, KP, CB, KP, CB)
        .transpose(0, 1, 2, 4, 3, 5)
        .reshape(-1, CB, CB)
    )
    first = jnp.broadcast_to(p_cols[:, None, :, None], (local_rows, KA, KP, KP)).reshape(-1)
    second = jnp.broadcast_to(ghost_c[:, :, None, :], (local_rows, KA, KP, KP)).reshape(-1)
    alive = jnp.broadcast_to(a_live[:, :, None, None] > 0, (local_rows, KA, KP, KP)).reshape(-1)
    owner = first // col_count * col_count + second % col_count
    spot = first % col_count * row_count + second // col_count
    order = jnp.arange(owner.shape[0], dtype=jnp.int32)
    earlier = (
        (owner[None, :] == owner[:, None]) & alive[None, :] & (order[None, :] < order[:, None])
    )
    rank = jnp.sum(earlier.astype(jnp.int32), axis=1)
    row_cap = max(2, -(-(local_rows * KP) // row_count))
    slot_cap = row_cap * max(1, KA * KP // col_count)
    slot = jnp.where(alive, owner * slot_cap + rank, dev_count * slot_cap)
    sent_blocks = jax.ops.segment_sum(partial_value, slot, num_segments=dev_count * slot_cap + 1)[
        :-1
    ]
    sent_spots = jax.ops.segment_sum(
        (spot + 1).astype(jnp.float32), slot, num_segments=dev_count * slot_cap + 1
    )[:-1]
    got_blocks, got_spots = (
        lax.all_to_all(
            sent_blocks.reshape(dev_count, slot_cap, CB, CB),
            ("row", "col"),
            split_axis=0,
            concat_axis=0,
            tiled=True,
        ),
        lax.all_to_all(
            sent_spots.reshape(dev_count, slot_cap),
            ("row", "col"),
            split_axis=0,
            concat_axis=0,
            tiled=True,
        ),
    )
    places = got_spots.reshape(-1).astype(jnp.int32) - 1
    places = jnp.where(places < 0, dev_count, places)
    summed = jax.ops.segment_sum(
        got_blocks.reshape(-1, CB, CB), places, num_segments=dev_count + 1
    )[:-1]
    coarse = (
        summed.reshape(col_count, row_count, CB, CB)
        .transpose(0, 2, 1, 3)
        .reshape(col_count * CB, row_count, 1, CB)
    )
    matrix = coarse.reshape(col_count * CB, row_count * CB)
    own_block = lax.dynamic_slice(matrix, (col_here * CB, row_here * CB), (CB, CB))
    floor_diag = jnp.maximum(jnp.abs(jnp.diagonal(own_block)), 1.0)
    current = guess
    for sweep in range(2):
        gathered = lax.all_gather(current, "row", axis=0, tiled=True)
        applied = lax.psum_scatter(
            jnp.dot(matrix, gathered, precision=highest), "col", scatter_dimension=0, tiled=True
        )
        current = current + damping * (rhs - applied) / floor_diag[:, None]
    return (coarse, current)


MESH = pl.DeviceIdType.MESH
QUOT = KA
TAKEN = 2 * KA


def halves(value):
    high = value.astype(jnp.bfloat16)
    return high, (value - high.astype(jnp.float32)).astype(jnp.bfloat16)


def beside(value):
    high, low = halves(value)
    return jnp.concatenate([high, high, low], axis=1)


def below(value):
    high, low = halves(value)
    return jnp.concatenate([high, low, high], axis=0)


def dot(left, right):
    return jnp.dot(left, right, preferred_element_type=jnp.float32)


def spread(value, names, count):
    parts = []
    for group in range(count):
        part = 0.0
        for m, name in enumerate(names):
            part = part + jnp.where(name == group, value[:, m * CB : (m + 1) * CB], 0.0)
        parts.append(part)
    return jnp.concatenate(parts, axis=1)


def kernel(
    rows, cols, a_ref, p_ref, meta_ref, own_ref, place_ref, live_ref, policy_ref, rate_ref,
    rhs_ref, guess_ref,
    matrix, out_ref,
    pall, part, got, ecat, products, abuf0, abuf1, metas, meta_s, x_all, x_wide, r_out, r_in,
    a_sem, l_sem, p_send, p_recv, m_send, m_recv, z_send, z_recv, s_send, s_recv,
    x_send, x_recv, r_send, r_recv,
):
    q = lax.axis_index("row")
    c = lax.axis_index("col")
    last = rows - 1
    blocks = pall.shape[1]
    digit_y, digit_x, core = c // 4, (c // 2) % 2, c % 2
    other = 1 - core
    swap_y, swap_x, swap_c = 1 - 2 * digit_y, 1 - 2 * digit_x, 1 - 2 * core

    def peer(flips):
        return c + flips[0] * swap_y * 4 + flips[1] * swap_x * 2 + flips[2] * swap_c

    to_flips = [
        (0, 0, 0), (0, 0, 1), (core, other, 0), (other, core, 1),
        (other, core, 0), (core, other, 1), (1, 1, 0), (1, 1, 1),
    ]
    from_flips = list(to_flips)
    from_flips[3], from_flips[5] = to_flips[5], to_flips[3]
    target = [peer(flips) for flips in to_flips]
    origin = [peer(flips) for flips in from_flips]
    plain = [peer((f // 4, (f // 2) % 2, f % 2)) for f in range(cols)]
    slot_k = [lax.rem(c - e + cols, cols) for e in target]
    abufs = [abuf0, abuf1]

    def remote(src, dst, send, recv, row, col):
        return pltpu.make_async_remote_copy(
            src_ref=src, dst_ref=dst, send_sem=send, recv_sem=recv,
            device_id=(row, col), device_id_type=MESH,
        )

    def load_a(t):
        return pltpu.make_async_copy(
            a_ref.at[:, slot_k[t]], abufs[t % 2], a_sem.at[t % 2]
        )

    own_p = pltpu.make_async_copy(p_ref, pall.at[0], l_sem.at[0])
    own_p.start()
    load_a(0).start()
    own_meta = pltpu.make_async_copy(meta_ref, metas.at[c], l_sem.at[1])
    own_meta.start()
    own_x = pltpu.make_async_copy(guess_ref, x_all.at[0, q], l_sem.at[2])
    own_x.start()

    barrier = pltpu.get_barrier_semaphore()
    for f in range(1, cols):
        pl.semaphore_signal(barrier, inc=1, device_id=(q, plain[f]), device_id_type=MESH)
    row_peer = [lax.rem(q + step, rows) for step in range(rows)]
    for step in range(1, rows):
        pl.semaphore_signal(barrier, inc=1, device_id=(row_peer[step], c), device_id_type=MESH)
    pl.semaphore_wait(barrier, cols - 1 + rows - 1)

    mid = blocks // 2
    p_copies = [
        remote(p_ref, pall.at[1], p_send.at[0], p_recv.at[0], q, target[1]),
        remote(p_ref, pall.at[2], p_send.at[1], p_recv.at[1], q, target[2]),
        remote(p_ref, pall.at[4], p_send.at[2], p_recv.at[2], q, target[4]),
        remote(pall.at[2], pall.at[3], p_send.at[3], p_recv.at[3], q, target[1]),
        remote(pall.at[4], pall.at[5], p_send.at[4], p_recv.at[4], q, target[1]),
        remote(
            pall.at[4, pl.ds(0, mid)], pall.at[6, pl.ds(0, mid)],
            p_send.at[5], p_recv.at[5], q, target[2],
        ),
        remote(
            pall.at[2, pl.ds(mid, blocks - mid)], pall.at[6, pl.ds(mid, blocks - mid)],
            p_send.at[6], p_recv.at[6], q, target[4],
        ),
        remote(pall.at[6], pall.at[7], p_send.at[7], p_recv.at[7], q, target[1]),
    ]
    m_copies = [
        remote(meta_ref, metas.at[c], m_send.at[f], m_recv.at[f], q, plain[f])
        for f in range(1, cols)
    ]

    p_copies[0].start()
    p_copies[1].start()
    for copy in m_copies:
        copy.start()

    def x_copies(sweep):
        return [
            remote(
                x_all.at[sweep, q], x_all.at[sweep, q],
                x_send.at[sweep, step], x_recv.at[sweep, step], row_peer[step], c,
            )
            for step in range(1, rows)
        ]

    own_p.wait()

    def p_block(t, j):
        return jnp.concatenate(
            [pall[t, j, pl.ds(m, BS, stride=KP), :] for m in range(KP)], axis=1
        )

    def widen(s, _):
        ecat[s] = beside(p_block(0, s).T)
        return 0

    lax.fori_loop(0, blocks, widen, 0)

    eye = lax.broadcasted_iota(jnp.int32, (BS, BS), 0) == lax.broadcasted_iota(
        jnp.int32, (BS, BS), 1
    )

    def compute(t):
        load_a(t).wait()
        if t + 1 < KA:
            load_a(t + 1).start()
        abuf = abufs[t % 2]

        def one(j, _):
            if t == 0:
                s = j
                names = [own_ref[j, m] for m in range(KP)]
            else:
                s = meta_s[target[t], j, slot_k[t] - 1]
                names = [meta_s[target[t], j, QUOT + m] for m in range(KP)]
            block = abuf[s] * live_ref[s, slot_k[t]].astype(jnp.float32)
            if t == 0:
                block = block + jnp.where(eye, rate_ref[pl.ds(policy_ref[j], 1), :], 0.0)
            product = dot(beside(block), below(p_block(t, j)))
            product = spread(dot(ecat[s], below(product)), names, rows)
            for m in range(KP):
                products[KP * j + m] = product[m * CB : (m + 1) * CB]
            return 0

        lax.fori_loop(0, blocks, one, 0)
        for group in range(rows):
            total = None
            for rank in range(blocks * KP // rows):
                s = place_ref[group, 2 * rank]
                m = place_ref[group, 2 * rank + 1]
                j = s if t == 0 else meta_s[target[t], s, TAKEN + slot_k[t] - 1]
                one_of = products[KP * j + m]
                total = one_of if total is None else total + one_of
            part[t, group] = total

    def z_copy(t, up, away, source):
        group = q + away if up else q - away
        to_row = q + 1 if up else q - 1
        slot = rows if (not up and away == 1) else group
        return remote(
            source.at[t, group], got.at[t, slot],
            z_send.at[t, int(up), away], z_recv.at[t, slot], to_row, c,
        )

    def z_got(t, slot):
        return remote(
            got.at[t, slot], got.at[t, slot],
            z_send.at[t, 0, 0], z_recv.at[t, slot], q, c,
        )

    def z_start(t):
        for away in range(last, 0, -1):
            for up in (True, False):
                @pl.when(q == (0 if up else last))
                def _():
                    z_copy(t, up, away, part).start()

    def z_pass(t):
        for away in range(last - 1, 0, -1):
            for up in (True, False):
                inside = (q > 0) & (q + away <= last) if up else (q < last) & (q - away >= 0)

                @pl.when(inside)
                def _():
                    group = q + away if up else q - away
                    z_got(t, group).wait_recv()
                    got[t, group] = got[t, group] + part[t, group]
                    z_copy(t, up, away, got).start()

    def z_wait(t):
        for away in range(1, rows):
            for up in (True, False):
                there = (q + away <= last) if up else (q - away >= 0)

                @pl.when(there)
                def _():
                    z_copy(t, up, away, part).wait_send()

    def strip_copy(t):
        return remote(
            part.at[t, q], matrix.at[c], s_send.at[t], s_recv.at[t], q, target[t]
        )

    def finish(t):
        @pl.when(q > 0)
        def _():
            z_got(t, q).wait_recv()
            part[t, q] = part[t, q] + got[t, q]

        @pl.when(q < last)
        def _():
            z_got(t, rows).wait_recv()
            part[t, q] = part[t, q] + got[t, rows]

        if t == 0:
            matrix[c] = part[0, q]
        else:
            strip_copy(t).start()

    def r_copy(sweep, t):
        return remote(
            r_out.at[sweep, t], r_in.at[sweep, t],
            r_send.at[sweep, t], r_recv.at[sweep, t], q, origin[t],
        )

    def apply_strip(sweep, t):
        if sweep == 0 and t > 0:
            strip_copy(t).wait_recv()
        r_out[sweep, t] = dot(beside(matrix[origin[t]]), x_wide[...])
        if t > 0:
            r_copy(sweep, t).start()

    for t in range(KA):
        if t == 1:
            own_meta.wait()
            for copy in m_copies:
                copy.wait_recv()
            to_smem = pltpu.make_async_copy(metas, meta_s, l_sem.at[3])
            to_smem.start()
            to_smem.wait()
            p_copies[0].wait_recv()
        if t == 2:
            p_copies[1].wait_recv()
            p_copies[3].start()
            p_copies[1].wait_send()
            p_copies[2].start()
        if t == 3:
            p_copies[3].wait_recv()
        if t == 4:
            p_copies[2].wait_recv()
            p_copies[4].start()
            p_copies[2].wait_send()
            p_copies[5].start()
            p_copies[6].start()
        if t == 5:
            p_copies[4].wait_recv()
        if t == 6:
            p_copies[5].wait_recv()
            p_copies[6].wait_recv()
            p_copies[7].start()
        if t == 7:
            p_copies[7].wait_recv()
        compute(t)
        z_start(t)
        if t == 1:
            own_x.wait()
            for copy in x_copies(0):
                copy.start()
        if t >= 1:
            z_pass(t - 1)
        if t >= 2:
            finish(t - 2)
        if t == 3:
            for copy in x_copies(0):
                copy.wait_recv()
            x_wide[...] = below(x_all[0].reshape(rows * CB, x_all.shape[3]))
        if t >= 3:
            apply_strip(0, t - 3)
    z_pass(KA - 1)
    finish(KA - 2)
    apply_strip(0, KA - 3)
    finish(KA - 1)
    apply_strip(0, KA - 2)
    apply_strip(0, KA - 1)
    same = lax.broadcasted_iota(jnp.int32, (CB, CB), 0) == lax.broadcasted_iota(
        jnp.int32, (CB, CB), 1
    )
    diagonal = jnp.zeros((CB, 1), jnp.float32)
    for group in range(rows):
        block = matrix[c, :, group * CB : (group + 1) * CB]
        kept = jnp.where(same & (q == group), block, 0.0)
        diagonal = diagonal + jnp.sum(kept, axis=1, keepdims=True)
    scale = damping / jnp.maximum(jnp.abs(diagonal), 1.0)

    current = guess_ref[...]
    for sweep in range(2):
        if sweep == 1:
            x_all[1, q] = current
            for copy in x_copies(1):
                copy.start()
            for copy in x_copies(1):
                copy.wait_recv()
            x_wide[...] = below(x_all[1].reshape(rows * CB, x_all.shape[3]))
            for t in range(KA - 1, -1, -1):
                apply_strip(1, t)
        applied = r_out[sweep, 0]
        for t in range(1, KA):
            r_copy(sweep, t).wait_recv()
            applied = applied + r_in[sweep, t]
        current = current + scale * (rhs_ref[...] - applied)
    out_ref[...] = current

    for copy in p_copies + m_copies + x_copies(0) + x_copies(1):
        if copy is not p_copies[1] and copy is not p_copies[2]:
            copy.wait_send()
    for t in range(KA):
        z_wait(t)
        if t > 0:
            strip_copy(t).wait_send()
            r_copy(0, t).wait_send()
            r_copy(1, t).wait_send()


def col_mesh(a_blocks, a_live, p_blocks, p_cols, ghost_list, policy, rates, rhs, guess):
    rows = lax.axis_size("row")
    cols = lax.axis_size("col")
    blocks = a_blocks.shape[0]
    width = rhs.shape[1]
    own_p = p_blocks.reshape(blocks, BS * KP, CB)
    order = jnp.arange(blocks, dtype=jnp.int32)
    held_at = jnp.sum(
        jnp.where(ghost_list[:, None, :] == order[None, :, None], order[:, None, None], 0), axis=0
    )
    names = p_cols // cols
    meta = jnp.concatenate(
        [
            jnp.pad(held_at, ((0, 0), (0, QUOT - held_at.shape[1]))),
            jnp.pad(names, ((0, 0), (0, TAKEN - QUOT - KP))),
            jnp.pad(ghost_list, ((0, 0), (0, CB - TAKEN - ghost_list.shape[1]))),
        ],
        axis=1,
    )
    flat = names.reshape(-1)
    entry = jnp.arange(flat.shape[0], dtype=jnp.int32)
    earlier = (flat[:, None] == flat[None, :]) & (entry[None, :] < entry[:, None])
    rank = jnp.sum(earlier.astype(jnp.int32), axis=1)
    group = jnp.arange(rows, dtype=jnp.int32)[:, None, None]
    place = jnp.arange(flat.shape[0] // rows, dtype=jnp.int32)[None, :, None]
    chosen = (flat == group) & (rank == place)
    parts = jnp.stack([entry // KP, entry % KP], axis=0)
    places = jnp.sum(jnp.where(chosen[:, :, None, :], parts, 0), axis=3).reshape(rows, -1)
    vmem = pl.BlockSpec(memory_space=pltpu.VMEM)
    smem = pl.BlockSpec(memory_space=pltpu.SMEM)
    anywhere = pl.BlockSpec(memory_space=pl.ANY)
    f32, bf16 = jnp.float32, jnp.bfloat16
    dma = pltpu.SemaphoreType.DMA
    matrix, smoothed = pl.pallas_call(
        functools.partial(kernel, rows, cols),
        out_shape=(
            jax.ShapeDtypeStruct((cols, CB, rows * CB), f32),
            jax.ShapeDtypeStruct((CB, width), f32),
        ),
        in_specs=[anywhere, anywhere, vmem, smem, smem, smem, smem, vmem, vmem, vmem],
        out_specs=(vmem, vmem),
        scratch_shapes=[
            pltpu.VMEM((KA, blocks, BS * KP, CB), f32),
            pltpu.VMEM((KA, rows, CB, rows * CB), f32),
            pltpu.VMEM((KA, rows + 1, CB, rows * CB), f32),
            pltpu.VMEM((blocks, KP * CB, 3 * BS), bf16),
            pltpu.VMEM((blocks * KP, CB, rows * CB), f32),
            pltpu.VMEM((blocks, BS, BS), f32),
            pltpu.VMEM((blocks, BS, BS), f32),
            pltpu.VMEM((cols, blocks, CB), jnp.int32),
            pltpu.SMEM((cols, blocks, CB), jnp.int32),
            pltpu.VMEM((2, rows, CB, width), f32),
            pltpu.VMEM((3 * rows * CB, width), bf16),
            pltpu.VMEM((2, KA, CB, width), f32),
            pltpu.VMEM((2, KA, CB, width), f32),
            dma((2,)), dma((4,)), dma((8,)), dma((8,)), dma((cols,)), dma((cols,)),
            dma((KA, 2, rows)), dma((KA, rows + 1)), dma((KA,)), dma((KA,)),
            dma((2, rows)), dma((2, rows)), dma((2, KA)), dma((2, KA)),
        ],
        compiler_params=pltpu.CompilerParams(
            collective_id=0, has_side_effects=True, vmem_limit_bytes=60 * 1024 * 1024
        ),
        cost_estimate=pl.CostEstimate(
            flops=12 * KA * blocks * BS * BS * BS,
            bytes_accessed=4 * (a_blocks.size + p_blocks.size), transcendentals=0,
        ),
        name="coarse_and_sweeps",
    )(a_blocks, own_p, meta, names, places, a_live, policy, rates, rhs, guess)
    return matrix.reshape(cols * CB, rows, 1, CB), smoothed


def on_device(a_blocks, *rest):
    if lax.axis_size("col") == a_blocks.shape[1]:
        return col_mesh(a_blocks, *rest)
    return any_mesh(a_blocks, *rest)


def solution(mesh):
    return jax.shard_map(
        on_device,
        mesh=mesh,
        in_specs=(
            P(("row", "col"), None, None, None),
            P(("row", "col"), None),
            P(("row", "col"), None, None, None),
            P(("row", "col"), None),
            P(("row", "col"), None),
            P(("row", "col")),
            P(),
            P(("row", "col"), None),
            P(("row", "col"), None),
        ),
        out_specs=(P("row", None, "col", None), P(("row", "col"), None)),
        check_vma=False,
    )
```

```python
import functools

import jax
import jax.numpy as jnp
from jax import lax
from jax.experimental import pallas as pl
from jax.experimental.pallas import tpu as pltpu
from jax.sharding import PartitionSpec as P

BS = 256
CB = 128
KA = 8
KP = 2
NPOL = 16


damping = 0.7


def from_behind(value, axis, steps):
    count = lax.axis_size(axis)
    pairs = [(source, (source + steps) % count) for source in range(count)]
    return lax.ppermute(value, axis, pairs)


def any_mesh(a_blocks, a_live, p_blocks, p_cols, ghost_list, policy, rates, rhs, guess):
    highest = lax.Precision.HIGHEST
    row_count = lax.axis_size("row")
    col_count = lax.axis_size("col")
    dev_count = row_count * col_count
    row_here = lax.axis_index("row")
    col_here = lax.axis_index("col")
    local_rows = a_blocks.shape[0]
    own_p = p_blocks.reshape(local_rows, BS, KP * CB)
    send_p = []
    send_c = []
    for offset in range(1, KA):
        picks = ghost_list[:, offset - 1]
        send_p.append(own_p[picks])
        send_c.append(p_cols[picks].astype(jnp.float32))
    incoming_p = [own_p]
    incoming_c = [p_cols]
    for offset in range(1, KA):
        moved_p, moved_c = from_behind((send_p[offset - 1], send_c[offset - 1]), "col", offset)
        incoming_p.append(moved_p)
        incoming_c.append(moved_c.astype(jnp.int32))
    ghost_p = jnp.stack(incoming_p, axis=1)
    ghost_c = jnp.stack(incoming_c, axis=1)
    live = a_live.astype(jnp.float32)
    selector = (policy[:, None] == jnp.arange(NPOL, dtype=jnp.int32)[None, :]).astype(jnp.float32)
    rate_rows = jnp.dot(selector, rates, precision=highest)
    product = jnp.einsum("skab,skbn->skan", a_blocks, ghost_p, precision=highest)
    product = product * live[:, :, None, None]
    product = product.at[:, 0].add(rate_rows[:, :, None] * own_p)
    partial_value = jnp.einsum("sam,skan->skmn", own_p, product, precision=highest)
    partial_value = (
        partial_value.reshape(local_rows, KA, KP, CB, KP, CB)
        .transpose(0, 1, 2, 4, 3, 5)
        .reshape(-1, CB, CB)
    )
    first = jnp.broadcast_to(p_cols[:, None, :, None], (local_rows, KA, KP, KP)).reshape(-1)
    second = jnp.broadcast_to(ghost_c[:, :, None, :], (local_rows, KA, KP, KP)).reshape(-1)
    alive = jnp.broadcast_to(a_live[:, :, None, None] > 0, (local_rows, KA, KP, KP)).reshape(-1)
    owner = first // col_count * col_count + second % col_count
    spot = first % col_count * row_count + second // col_count
    order = jnp.arange(owner.shape[0], dtype=jnp.int32)
    earlier = (
        (owner[None, :] == owner[:, None]) & alive[None, :] & (order[None, :] < order[:, None])
    )
    rank = jnp.sum(earlier.astype(jnp.int32), axis=1)
    row_cap = max(2, -(-(local_rows * KP) // row_count))
    slot_cap = row_cap * max(1, KA * KP // col_count)
    slot = jnp.where(alive, owner * slot_cap + rank, dev_count * slot_cap)
    sent_blocks = jax.ops.segment_sum(partial_value, slot, num_segments=dev_count * slot_cap + 1)[
        :-1
    ]
    sent_spots = jax.ops.segment_sum(
        (spot + 1).astype(jnp.float32), slot, num_segments=dev_count * slot_cap + 1
    )[:-1]
    got_blocks, got_spots = (
        lax.all_to_all(
            sent_blocks.reshape(dev_count, slot_cap, CB, CB),
            ("row", "col"),
            split_axis=0,
            concat_axis=0,
            tiled=True,
        ),
        lax.all_to_all(
            sent_spots.reshape(dev_count, slot_cap),
            ("row", "col"),
            split_axis=0,
            concat_axis=0,
            tiled=True,
        ),
    )
    places = got_spots.reshape(-1).astype(jnp.int32) - 1
    places = jnp.where(places < 0, dev_count, places)
    summed = jax.ops.segment_sum(
        got_blocks.reshape(-1, CB, CB), places, num_segments=dev_count + 1
    )[:-1]
    coarse = (
        summed.reshape(col_count, row_count, CB, CB)
        .transpose(0, 2, 1, 3)
        .reshape(col_count * CB, row_count, 1, CB)
    )
    matrix = coarse.reshape(col_count * CB, row_count * CB)
    own_block = lax.dynamic_slice(matrix, (col_here * CB, row_here * CB), (CB, CB))
    floor_diag = jnp.maximum(jnp.abs(jnp.diagonal(own_block)), 1.0)
    current = guess
    for sweep in range(2):
        gathered = lax.all_gather(current, "row", axis=0, tiled=True)
        applied = lax.psum_scatter(
            jnp.dot(matrix, gathered, precision=highest), "col", scatter_dimension=0, tiled=True
        )
        current = current + damping * (rhs - applied) / floor_diag[:, None]
    return (coarse, current)


MESH = pl.DeviceIdType.MESH
QUOT = KA
MEET = {1: 0, 3: 4, 5: 2, 7: 6}
LATE = [0, 1, 6, 7, 2, 3, 4, 5]


def halves(value):
    high = value.astype(jnp.bfloat16)
    return high, (value - high.astype(jnp.float32)).astype(jnp.bfloat16)


def beside(value):
    high, low = halves(value)
    return jnp.concatenate([high, high, low], axis=1)


def below(value):
    high, low = halves(value)
    return jnp.concatenate([high, low, high], axis=0)


def dot(left, right):
    return jnp.dot(left, right, preferred_element_type=jnp.float32)


def spread(value, names, count):
    parts = []
    for group in range(count):
        part = 0.0
        for m, name in enumerate(names):
            part = part + jnp.where(name == group, value[:, m * CB : (m + 1) * CB], 0.0)
        parts.append(part)
    return jnp.concatenate(parts, axis=1)


def kernel(
    rows, cols, a_ref, p_ref, taken_ref, cols_ref, own_ref, live_ref, policy_ref, rate_ref,
    rhs_ref, guess_ref,
    matrix, out_ref,
    pall, part, got, ecat, products, abuf0, abuf1, meta_ref, metas, meta_s, x_all, x_wide, r_out, r_near, r_in,
    a_sem, l_sem, p_send, p_recv, m_send, m_recv, z_send, z_recv, s_send, s_recv,
    x_send, x_recv, r_send, r_recv, n_send, n_recv,
):
    q = lax.axis_index("row")
    c = lax.axis_index("col")
    last = rows - 1
    blocks = pall.shape[1]
    digit_y, digit_x, core = c // 4, (c // 2) % 2, c % 2
    other = 1 - core
    swap_y, swap_x, swap_c = 1 - 2 * digit_y, 1 - 2 * digit_x, 1 - 2 * core

    def peer(flips):
        return c + flips[0] * swap_y * 4 + flips[1] * swap_x * 2 + flips[2] * swap_c

    to_flips = [
        (0, 0, 0), (0, 0, 1), (core, other, 0), (other, core, 1),
        (other, core, 0), (core, other, 1), (1, 1, 0), (1, 1, 1),
    ]
    from_flips = list(to_flips)
    from_flips[3], from_flips[5] = to_flips[5], to_flips[3]
    target = [peer(flips) for flips in to_flips]
    origin = [peer(flips) for flips in from_flips]
    plain = [peer((f // 4, (f // 2) % 2, f % 2)) for f in range(cols)]
    slot_k = [lax.rem(c - e + cols, cols) for e in target]
    abufs = [abuf0, abuf1]

    def remote(src, dst, send, recv, row, col):
        return pltpu.make_async_remote_copy(
            src_ref=src, dst_ref=dst, send_sem=send, recv_sem=recv,
            device_id=(row, col), device_id_type=MESH,
        )

    def load_a(t):
        return pltpu.make_async_copy(
            a_ref.at[:, slot_k[t]], abufs[t % 2], a_sem.at[t % 2]
        )

    own_p = pltpu.make_async_copy(p_ref, pall.at[0], l_sem.at[0])
    own_p.start()
    load_a(0).start()
    meta_ref[...] = jnp.zeros_like(meta_ref)
    meta_ref[0 : KA - 1, 0:blocks] = taken_ref[...]
    meta_ref[QUOT : QUOT + KP, 0:blocks] = cols_ref[...]
    own_meta = pltpu.make_async_copy(meta_ref, metas.at[c], l_sem.at[1])
    own_meta.start()
    own_x = pltpu.make_async_copy(guess_ref, x_all.at[0, q], l_sem.at[2])
    own_x.start()

    barrier = pltpu.get_barrier_semaphore()
    for f in range(1, cols):
        pl.semaphore_signal(barrier, inc=1, device_id=(q, plain[f]), device_id_type=MESH)
    row_peer = [lax.rem(q + step, rows) for step in range(rows)]
    for step in range(1, rows):
        pl.semaphore_signal(barrier, inc=1, device_id=(row_peer[step], c), device_id_type=MESH)
    pl.semaphore_wait(barrier, cols - 1 + rows - 1)

    mid = blocks // 2
    p_copies = [
        remote(p_ref, pall.at[1], p_send.at[0], p_recv.at[0], q, target[1]),
        remote(p_ref, pall.at[2], p_send.at[1], p_recv.at[1], q, target[2]),
        remote(p_ref, pall.at[4], p_send.at[2], p_recv.at[2], q, target[4]),
        remote(pall.at[2], pall.at[3], p_send.at[3], p_recv.at[3], q, target[1]),
        remote(pall.at[4], pall.at[5], p_send.at[4], p_recv.at[4], q, target[1]),
        remote(
            pall.at[4, pl.ds(0, mid)], pall.at[6, pl.ds(0, mid)],
            p_send.at[5], p_recv.at[5], q, target[2],
        ),
        remote(
            pall.at[2, pl.ds(mid, blocks - mid)], pall.at[6, pl.ds(mid, blocks - mid)],
            p_send.at[6], p_recv.at[6], q, target[4],
        ),
        remote(pall.at[6], pall.at[7], p_send.at[7], p_recv.at[7], q, target[1]),
    ]
    m_copies = [
        remote(meta_ref, metas.at[c], m_send.at[f], m_recv.at[f], q, plain[f])
        for f in range(1, cols)
    ]

    p_copies[0].start()
    p_copies[1].start()
    for copy in m_copies:
        copy.start()
    own_x.wait()

    def x_copies(sweep):
        return [
            remote(
                x_all.at[sweep, q], x_all.at[sweep, q],
                x_send.at[sweep, step], x_recv.at[sweep, step], row_peer[step], c,
            )
            for step in range(1, rows)
        ]

    for copy in x_copies(0):
        copy.start()
    own_p.wait()

    own_names = [[lax.div(own_ref[m, j], cols) for m in range(KP)] for j in range(blocks)]
    places = []
    for group in range(rows):
        found = 0
        slots = [(0, 0)] * (blocks * KP // rows)
        for j in range(blocks):
            for m in range(KP):
                hit = own_names[j][m] == group
                slots = [
                    (
                        jnp.where(hit & (found == rank), j, held[0]),
                        jnp.where(hit & (found == rank), m, held[1]),
                    )
                    for rank, held in enumerate(slots)
                ]
                found = found + hit.astype(jnp.int32)
        places.append(slots)

    def p_block(t, j):
        return jnp.concatenate(
            [pall[t, j, pl.ds(m, BS, stride=KP), :] for m in range(KP)], axis=1
        )

    def widen(s, _):
        ecat[s] = beside(p_block(0, s).T)
        return 0

    lax.fori_loop(0, blocks, widen, 0)

    eye = lax.broadcasted_iota(jnp.int32, (BS, BS), 0) == lax.broadcasted_iota(
        jnp.int32, (BS, BS), 1
    )

    def compute(t):
        load_a(t).wait()
        if t + 1 < KA:
            load_a(t + 1).start()
        abuf = abufs[t % 2]

        def one(j, _):
            if t == 0:
                s = j
                names = [lax.div(own_ref[m, j], cols) for m in range(KP)]
            else:
                s = 0
                for held in range(blocks):
                    taken = meta_s[target[t], slot_k[t] - 1, held]
                    s = jnp.where(taken == j, held, s)
                names = [lax.div(meta_s[target[t], QUOT + m, j], cols) for m in range(KP)]
            block = abuf[s] * live_ref[s, slot_k[t]].astype(jnp.float32)
            if t == 0:
                block = block + jnp.where(eye, rate_ref[pl.ds(policy_ref[j], 1), :], 0.0)
            product = dot(beside(block), below(p_block(t, j)))
            product = spread(dot(ecat[s], below(product)), names, rows)
            for m in range(KP):
                products[KP * j + m] = product[m * CB : (m + 1) * CB]
            return 0

        lax.fori_loop(0, blocks, one, 0)
        for group in range(rows):
            total = None
            for s, m in places[group]:
                j = s if t == 0 else meta_s[target[t], slot_k[t] - 1, s]
                one_of = products[KP * j + m]
                total = one_of if total is None else total + one_of
            part[t, group] = total

    def z_copy(t, up, away, source):
        group = q + away if up else q - away
        to_row = q + 1 if up else q - 1
        slot = rows if (not up and away == 1) else group
        return remote(
            source.at[t, group], got.at[t, slot],
            z_send.at[t, int(up), away], z_recv.at[t, slot], to_row, c,
        )

    def z_got(t, slot):
        return remote(
            got.at[t, slot], got.at[t, slot],
            z_send.at[t, 0, 0], z_recv.at[t, slot], q, c,
        )

    def z_start(t, ways):
        for away in ways:
            for up in (True, False):
                @pl.when(q == (0 if up else last))
                def _():
                    z_copy(t, up, away, part).start()

    def z_pass(t):
        for away in range(last - 1, 0, -1):
            for up in (True, False):
                inside = (q > 0) & (q + away <= last) if up else (q < last) & (q - away >= 0)

                @pl.when(inside)
                def _():
                    group = q + away if up else q - away
                    z_got(t, group).wait_recv()
                    got[t, group] = got[t, group] + part[t, group]
                    z_copy(t, up, away, got).start()

    def z_wait(t):
        for away in range(1, rows):
            for up in (True, False):
                there = (q + away <= last) if up else (q - away >= 0)
                if away == 1 and t in LATE[2 : KA - 2]:
                    there = there & (q != (0 if up else last))

                @pl.when(there)
                def _():
                    z_copy(t, up, away, part).wait_send()

    def near_wait(t):
        for up in (True, False):
            @pl.when(q == (0 if up else last))
            def _():
                z_copy(t, up, 1, part).wait_send()

    def strip_copy(t):
        return remote(
            part.at[t, q], matrix.at[c], s_send.at[t], s_recv.at[t], q, target[t]
        )

    def finish(t):
        @pl.when(q > 0)
        def _():
            z_got(t, q).wait_recv()
            part[t, q] = part[t, q] + got[t, q]

        @pl.when(q < last)
        def _():
            z_got(t, rows).wait_recv()
            part[t, q] = part[t, q] + got[t, rows]

        if t == 0:
            matrix[c] = part[0, q]
        else:
            strip_copy(t).start()

    def near_copy(sweep, t):
        return remote(
            r_out.at[sweep, t], r_near.at[sweep, MEET[t]],
            n_send.at[sweep, t], n_recv.at[sweep, MEET[t]], q, target[1],
        )

    def near_got(sweep, t):
        return remote(
            r_near.at[sweep, t], r_near.at[sweep, t],
            n_send.at[sweep, t], n_recv.at[sweep, t], q, target[1],
        )

    def r_copy(sweep, t):
        return remote(
            r_out.at[sweep, t], r_in.at[sweep, t],
            r_send.at[sweep, t], r_recv.at[sweep, t], q, target[t],
        )

    def apply_strip(sweep, t):
        if sweep == 0 and t > 0:
            strip_copy(t).wait_recv()
        r_out[sweep, t] = dot(beside(matrix[origin[t]]), x_wide[...])
        if t in MEET:
            near_copy(sweep, t).start()

    def combine(sweep, t):
        near_got(sweep, t).wait_recv()
        r_out[sweep, t] = r_out[sweep, t] + r_near[sweep, t]
        if t > 0:
            r_copy(sweep, t).start()

    for t in range(KA):
        if t == 1:
            own_meta.wait()
            for copy in m_copies:
                copy.wait_recv()
            to_smem = pltpu.make_async_copy(metas, meta_s, l_sem.at[3])
            to_smem.start()
            to_smem.wait()
            p_copies[0].wait_recv()
        if t == 2:
            p_copies[1].wait_recv()
            p_copies[3].start()
            p_copies[1].wait_send()
            p_copies[2].start()
        if t == 3:
            p_copies[3].wait_recv()
        if t == 4:
            p_copies[2].wait_recv()
            p_copies[4].start()
            p_copies[2].wait_send()
            p_copies[5].start()
            p_copies[6].start()
        if t == 5:
            p_copies[4].wait_recv()
        if t == 6:
            p_copies[5].wait_recv()
            p_copies[6].wait_recv()
            p_copies[7].start()
        if t == 7:
            p_copies[7].wait_recv()
        compute(t)
        z_start(t, range(last, 0, -1) if t in LATE[:2] else range(last, 1, -1))
        if t >= 1:
            z_pass(t - 1)
    z_start(LATE[2], [1])
    z_start(LATE[3], [1])
    z_pass(KA - 1)
    for copy in x_copies(0):
        copy.wait_recv()
    x_wide[...] = below(x_all[0].reshape(rows * CB, x_all.shape[3]))
    for i, t in enumerate(LATE):
        if i + 4 < KA:
            near_wait(LATE[i + 2])
            z_start(LATE[i + 4], [1])
        finish(t)
        if i >= 1:
            apply_strip(0, LATE[i - 1])
        if i == 5:
            combine(0, 6)
    apply_strip(0, LATE[KA - 1])
    for t in (4, 2, 0):
        combine(0, t)

    same = lax.broadcasted_iota(jnp.int32, (CB, CB), 0) == lax.broadcasted_iota(
        jnp.int32, (CB, CB), 1
    )
    diagonal = jnp.zeros((CB, 1), jnp.float32)
    for group in range(rows):
        block = matrix[c, :, group * CB : (group + 1) * CB]
        kept = jnp.where(same & (q == group), block, 0.0)
        diagonal = diagonal + jnp.sum(kept, axis=1, keepdims=True)
    scale = damping / jnp.maximum(jnp.abs(diagonal), 1.0)

    current = guess_ref[...]
    for sweep in range(2):
        if sweep == 1:
            x_all[1, q] = current
            for copy in x_copies(1):
                copy.start()
            for copy in x_copies(1):
                copy.wait_recv()
            x_wide[...] = below(x_all[1].reshape(rows * CB, x_all.shape[3]))
            for t in (7, 3, 5, 1, 6):
                apply_strip(1, t)
            combine(1, 6)
            apply_strip(1, 4)
            combine(1, 4)
            apply_strip(1, 2)
            combine(1, 2)
            apply_strip(1, 0)
            combine(1, 0)
        applied = r_out[sweep, 0]
        for t in (2, 4, 6):
            r_copy(sweep, t).wait_recv()
            applied = applied + r_in[sweep, t]
        current = current + scale * (rhs_ref[...] - applied)
    out_ref[...] = current

    for copy in p_copies + m_copies + x_copies(0) + x_copies(1):
        if copy is not p_copies[1] and copy is not p_copies[2]:
            copy.wait_send()
    for t in range(KA):
        z_wait(t)
        if t > 0:
            strip_copy(t).wait_send()
        for sweep in range(2):
            if t in MEET:
                near_copy(sweep, t).wait_send()
            elif t > 0:
                r_copy(sweep, t).wait_send()


def col_mesh(a_blocks, a_live, p_blocks, p_cols, ghost_list, policy, rates, rhs, guess):
    rows = lax.axis_size("row")
    cols = lax.axis_size("col")
    blocks = a_blocks.shape[0]
    width = rhs.shape[1]
    own_p = p_blocks.reshape(blocks, BS * KP, CB)
    vmem = pl.BlockSpec(memory_space=pltpu.VMEM)
    smem = pl.BlockSpec(memory_space=pltpu.SMEM)
    anywhere = pl.BlockSpec(memory_space=pl.ANY)
    f32, bf16 = jnp.float32, jnp.bfloat16
    dma = pltpu.SemaphoreType.DMA
    matrix, smoothed = pl.pallas_call(
        functools.partial(kernel, rows, cols),
        out_shape=(
            jax.ShapeDtypeStruct((cols, CB, rows * CB), f32),
            jax.ShapeDtypeStruct((CB, width), f32),
        ),
        in_specs=[anywhere, anywhere, vmem, vmem, smem, smem, smem, vmem, vmem, vmem],
        out_specs=(vmem, vmem),
        scratch_shapes=[
            pltpu.VMEM((KA, blocks, BS * KP, CB), f32),
            pltpu.VMEM((KA, rows, CB, rows * CB), f32),
            pltpu.VMEM((KA, rows + 1, CB, rows * CB), f32),
            pltpu.VMEM((blocks, KP * CB, 3 * BS), bf16),
            pltpu.VMEM((blocks * KP, CB, rows * CB), f32),
            pltpu.VMEM((blocks, BS, BS), f32),
            pltpu.VMEM((blocks, BS, BS), f32),
            pltpu.VMEM((2 * KA, CB), jnp.int32),
            pltpu.VMEM((cols, 2 * KA, CB), jnp.int32),
            pltpu.SMEM((cols, 2 * KA, CB), jnp.int32),
            pltpu.VMEM((2, rows, CB, width), f32),
            pltpu.VMEM((3 * rows * CB, width), bf16),
            pltpu.VMEM((2, KA, CB, width), f32),
            pltpu.VMEM((2, KA, CB, width), f32),
            pltpu.VMEM((2, KA, CB, width), f32),
            dma((2,)), dma((4,)), dma((8,)), dma((8,)), dma((cols,)), dma((cols,)),
            dma((KA, 2, rows)), dma((KA, rows + 1)), dma((KA,)), dma((KA,)),
            dma((2, rows)), dma((2, rows)), dma((2, KA)), dma((2, KA)), dma((2, KA)), dma((2, KA)),
        ],
        compiler_params=pltpu.CompilerParams(
            collective_id=0, has_side_effects=True, vmem_limit_bytes=60 * 1024 * 1024
        ),
        cost_estimate=pl.CostEstimate(
            flops=12 * KA * blocks * BS * BS * BS,
            bytes_accessed=4 * (a_blocks.size + p_blocks.size), transcendentals=0,
        ),
        name="coarse_and_sweeps",
    )(a_blocks, own_p, ghost_list.T, p_cols.T, p_cols.T, a_live, policy, rates, rhs, guess)
    return matrix.reshape(cols * CB, rows, 1, CB), smoothed


def on_device(a_blocks, *rest):
    if lax.axis_size("col") == a_blocks.shape[1]:
        return col_mesh(a_blocks, *rest)
    return any_mesh(a_blocks, *rest)


def solution(mesh):
    return jax.shard_map(
        on_device,
        mesh=mesh,
        in_specs=(
            P(("row", "col"), None, None, None),
            P(("row", "col"), None),
            P(("row", "col"), None, None, None),
            P(("row", "col"), None),
            P(("row", "col"), None),
            P(("row", "col")),
            P(),
            P(("row", "col"), None),
            P(("row", "col"), None),
        ),
        out_specs=(P("row", None, "col", None), P(("row", "col"), None)),
        check_vma=False,
    )
```

```python
import functools

import jax
import jax.numpy as jnp
from jax import lax
from jax.experimental import pallas as pl
from jax.experimental.pallas import tpu as pltpu
from jax.sharding import PartitionSpec as P

BS = 256
CB = 128
KA = 8
KP = 2
NPOL = 16


damping = 0.7


def from_behind(value, axis, steps):
    count = lax.axis_size(axis)
    pairs = [(source, (source + steps) % count) for source in range(count)]
    return lax.ppermute(value, axis, pairs)


def any_mesh(a_blocks, a_live, p_blocks, p_cols, ghost_list, policy, rates, rhs, guess):
    highest = lax.Precision.HIGHEST
    row_count = lax.axis_size("row")
    col_count = lax.axis_size("col")
    dev_count = row_count * col_count
    row_here = lax.axis_index("row")
    col_here = lax.axis_index("col")
    local_rows = a_blocks.shape[0]
    own_p = p_blocks.reshape(local_rows, BS, KP * CB)
    send_p = []
    send_c = []
    for offset in range(1, KA):
        picks = ghost_list[:, offset - 1]
        send_p.append(own_p[picks])
        send_c.append(p_cols[picks].astype(jnp.float32))
    incoming_p = [own_p]
    incoming_c = [p_cols]
    for offset in range(1, KA):
        moved_p, moved_c = from_behind((send_p[offset - 1], send_c[offset - 1]), "col", offset)
        incoming_p.append(moved_p)
        incoming_c.append(moved_c.astype(jnp.int32))
    ghost_p = jnp.stack(incoming_p, axis=1)
    ghost_c = jnp.stack(incoming_c, axis=1)
    live = a_live.astype(jnp.float32)
    selector = (policy[:, None] == jnp.arange(NPOL, dtype=jnp.int32)[None, :]).astype(jnp.float32)
    rate_rows = jnp.dot(selector, rates, precision=highest)
    product = jnp.einsum("skab,skbn->skan", a_blocks, ghost_p, precision=highest)
    product = product * live[:, :, None, None]
    product = product.at[:, 0].add(rate_rows[:, :, None] * own_p)
    partial_value = jnp.einsum("sam,skan->skmn", own_p, product, precision=highest)
    partial_value = (
        partial_value.reshape(local_rows, KA, KP, CB, KP, CB)
        .transpose(0, 1, 2, 4, 3, 5)
        .reshape(-1, CB, CB)
    )
    first = jnp.broadcast_to(p_cols[:, None, :, None], (local_rows, KA, KP, KP)).reshape(-1)
    second = jnp.broadcast_to(ghost_c[:, :, None, :], (local_rows, KA, KP, KP)).reshape(-1)
    alive = jnp.broadcast_to(a_live[:, :, None, None] > 0, (local_rows, KA, KP, KP)).reshape(-1)
    owner = first // col_count * col_count + second % col_count
    spot = first % col_count * row_count + second // col_count
    order = jnp.arange(owner.shape[0], dtype=jnp.int32)
    earlier = (
        (owner[None, :] == owner[:, None]) & alive[None, :] & (order[None, :] < order[:, None])
    )
    rank = jnp.sum(earlier.astype(jnp.int32), axis=1)
    row_cap = max(2, -(-(local_rows * KP) // row_count))
    slot_cap = row_cap * max(1, KA * KP // col_count)
    slot = jnp.where(alive, owner * slot_cap + rank, dev_count * slot_cap)
    sent_blocks = jax.ops.segment_sum(partial_value, slot, num_segments=dev_count * slot_cap + 1)[
        :-1
    ]
    sent_spots = jax.ops.segment_sum(
        (spot + 1).astype(jnp.float32), slot, num_segments=dev_count * slot_cap + 1
    )[:-1]
    got_blocks, got_spots = (
        lax.all_to_all(
            sent_blocks.reshape(dev_count, slot_cap, CB, CB),
            ("row", "col"),
            split_axis=0,
            concat_axis=0,
            tiled=True,
        ),
        lax.all_to_all(
            sent_spots.reshape(dev_count, slot_cap),
            ("row", "col"),
            split_axis=0,
            concat_axis=0,
            tiled=True,
        ),
    )
    places = got_spots.reshape(-1).astype(jnp.int32) - 1
    places = jnp.where(places < 0, dev_count, places)
    summed = jax.ops.segment_sum(
        got_blocks.reshape(-1, CB, CB), places, num_segments=dev_count + 1
    )[:-1]
    coarse = (
        summed.reshape(col_count, row_count, CB, CB)
        .transpose(0, 2, 1, 3)
        .reshape(col_count * CB, row_count, 1, CB)
    )
    matrix = coarse.reshape(col_count * CB, row_count * CB)
    own_block = lax.dynamic_slice(matrix, (col_here * CB, row_here * CB), (CB, CB))
    floor_diag = jnp.maximum(jnp.abs(jnp.diagonal(own_block)), 1.0)
    current = guess
    for sweep in range(2):
        gathered = lax.all_gather(current, "row", axis=0, tiled=True)
        applied = lax.psum_scatter(
            jnp.dot(matrix, gathered, precision=highest), "col", scatter_dimension=0, tiled=True
        )
        current = current + damping * (rhs - applied) / floor_diag[:, None]
    return (coarse, current)


MESH = pl.DeviceIdType.MESH
QUOT = KA
MEET = {1: 0, 3: 4, 5: 2, 7: 6}
LATE = [0, 1, 2, 3, 6, 7, 4, 5]


def halves(value):
    high = value.astype(jnp.bfloat16)
    return high, (value - high.astype(jnp.float32)).astype(jnp.bfloat16)


def beside(value):
    high, low = halves(value)
    return jnp.concatenate([high, high, low], axis=1)


def below(value):
    high, low = halves(value)
    return jnp.concatenate([high, low, high], axis=0)


def dot(left, right):
    return jnp.dot(left, right, preferred_element_type=jnp.float32)


def spread(value, names, count):
    parts = []
    for group in range(count):
        part = 0.0
        for m, name in enumerate(names):
            part = part + jnp.where(name == group, value[:, m * CB : (m + 1) * CB], 0.0)
        parts.append(part)
    return jnp.concatenate(parts, axis=1)


def kernel(
    rows, cols, a_ref, p_ref, taken_ref, cols_ref, own_ref, live_ref, policy_ref, rate_ref,
    rhs_ref, guess_ref,
    rows_ref, out_ref,
    pall, matrix, part, got, ecat, products, abuf0, abuf1, meta_ref, metas, meta_s, x_all, x_wide, r_out, r_near, r_in,
    a_sem, l_sem, p_send, p_recv, m_send, m_recv, z_send, z_recv, s_send, s_recv,
    x_send, x_recv, r_send, r_recv, n_send, n_recv, o_sem,
):
    q = lax.axis_index("row")
    c = lax.axis_index("col")
    last = rows - 1
    blocks = pall.shape[1]
    digit_y, digit_x, core = c // 4, (c // 2) % 2, c % 2
    other = 1 - core
    swap_y, swap_x, swap_c = 1 - 2 * digit_y, 1 - 2 * digit_x, 1 - 2 * core

    def peer(flips):
        return c + flips[0] * swap_y * 4 + flips[1] * swap_x * 2 + flips[2] * swap_c

    to_flips = [
        (0, 0, 0), (0, 0, 1), (core, other, 0), (other, core, 1),
        (other, core, 0), (core, other, 1), (1, 1, 0), (1, 1, 1),
    ]
    from_flips = list(to_flips)
    from_flips[3], from_flips[5] = to_flips[5], to_flips[3]
    target = [peer(flips) for flips in to_flips]
    origin = [peer(flips) for flips in from_flips]
    plain = [peer((f // 4, (f // 2) % 2, f % 2)) for f in range(cols)]
    slot_k = [lax.rem(c - e + cols, cols) for e in target]
    abufs = [abuf0, abuf1]

    def remote(src, dst, send, recv, row, col):
        return pltpu.make_async_remote_copy(
            src_ref=src, dst_ref=dst, send_sem=send, recv_sem=recv,
            device_id=(row, col), device_id_type=MESH,
        )

    def load_a(t):
        return pltpu.make_async_copy(
            a_ref.at[:, slot_k[t]], abufs[t % 2], a_sem.at[t % 2]
        )

    own_p = pltpu.make_async_copy(p_ref, pall.at[0], l_sem.at[0])
    own_p.start()
    load_a(0).start()
    meta_ref[...] = jnp.zeros_like(meta_ref)
    meta_ref[0:blocks, 0 : KA - 1] = taken_ref[...]
    meta_ref[QUOT : QUOT + KP, 0:blocks] = cols_ref[...]
    own_meta = pltpu.make_async_copy(meta_ref, metas.at[c], l_sem.at[1])
    own_meta.start()
    own_x = pltpu.make_async_copy(guess_ref, x_all.at[0, q], l_sem.at[2])
    own_x.start()

    barrier = pltpu.get_barrier_semaphore()
    for f in range(1, cols):
        pl.semaphore_signal(barrier, inc=1, device_id=(q, plain[f]), device_id_type=MESH)
    row_peer = [lax.rem(q + step, rows) for step in range(rows)]
    for step in range(1, rows):
        pl.semaphore_signal(barrier, inc=1, device_id=(row_peer[step], c), device_id_type=MESH)
    pl.semaphore_wait(barrier, cols - 1 + rows - 1)

    mid = blocks // 2
    p_copies = [
        remote(p_ref, pall.at[1], p_send.at[0], p_recv.at[0], q, target[1]),
        remote(p_ref, pall.at[2], p_send.at[1], p_recv.at[1], q, target[2]),
        remote(p_ref, pall.at[4], p_send.at[2], p_recv.at[2], q, target[4]),
        remote(pall.at[2], pall.at[3], p_send.at[3], p_recv.at[3], q, target[1]),
        remote(pall.at[4], pall.at[5], p_send.at[4], p_recv.at[4], q, target[1]),
        remote(
            pall.at[4, pl.ds(0, mid)], pall.at[6, pl.ds(0, mid)],
            p_send.at[5], p_recv.at[5], q, target[2],
        ),
        remote(
            pall.at[2, pl.ds(mid, blocks - mid)], pall.at[6, pl.ds(mid, blocks - mid)],
            p_send.at[6], p_recv.at[6], q, target[4],
        ),
        remote(pall.at[6], pall.at[7], p_send.at[7], p_recv.at[7], q, target[1]),
    ]
    m_copies = [
        remote(meta_ref, metas.at[c], m_send.at[f], m_recv.at[f], q, plain[f])
        for f in range(1, cols)
    ]

    p_copies[0].start()
    p_copies[1].start()
    for copy in m_copies:
        copy.start()
    own_x.wait()

    def x_copies(sweep):
        return [
            remote(
                x_all.at[sweep, q], x_all.at[sweep, q],
                x_send.at[sweep, step], x_recv.at[sweep, step], row_peer[step], c,
            )
            for step in range(1, rows)
        ]

    for copy in x_copies(0):
        copy.start()
    own_p.wait()

    own_names = [[lax.div(own_ref[m, j], cols) for m in range(KP)] for j in range(blocks)]
    places = []
    for group in range(rows):
        found = 0
        slots = [(0, 0)] * (blocks * KP // rows)
        for j in range(blocks):
            for m in range(KP):
                hit = own_names[j][m] == group
                slots = [
                    (
                        jnp.where(hit & (found == rank), j, held[0]),
                        jnp.where(hit & (found == rank), m, held[1]),
                    )
                    for rank, held in enumerate(slots)
                ]
                found = found + hit.astype(jnp.int32)
        places.append(slots)

    def p_block(t, j):
        return jnp.concatenate(
            [pall[t, j, pl.ds(m, BS, stride=KP), :] for m in range(KP)], axis=1
        )

    eye = lax.broadcasted_iota(jnp.int32, (BS, BS), 0) == lax.broadcasted_iota(
        jnp.int32, (BS, BS), 1
    )

    def compute(t):
        load_a(t).wait()
        if t + 1 < KA:
            load_a(t + 1).start()
        abuf = abufs[t % 2]

        def one(j, _):
            if t == 0:
                s = j
                ecat[j] = beside(p_block(0, j).T)
                names = [lax.div(own_ref[m, j], cols) for m in range(KP)]
            else:
                s = 0
                for held in range(blocks):
                    taken = meta_s[target[t], held, slot_k[t] - 1]
                    s = jnp.where(taken == j, held, s)
                names = [lax.div(meta_s[target[t], QUOT + m, j], cols) for m in range(KP)]
            block = abuf[s] * live_ref[s, slot_k[t]].astype(jnp.float32)
            if t == 0:
                block = block + jnp.where(eye, rate_ref[pl.ds(policy_ref[j], 1), :], 0.0)
            product = dot(beside(block), below(p_block(t, j)))
            product = spread(dot(ecat[s], below(product)), names, rows)
            for m in range(KP):
                products[KP * j + m] = product[m * CB : (m + 1) * CB]
            return 0

        lax.fori_loop(0, blocks, one, 0)
        for group in range(rows):
            total = None
            for s, m in places[group]:
                j = s if t == 0 else meta_s[target[t], s, slot_k[t] - 1]
                one_of = products[KP * j + m]
                total = one_of if total is None else total + one_of
            part[t, group] = total

    def z_copy(t, up, away, source):
        group = q + away if up else q - away
        to_row = q + 1 if up else q - 1
        slot = rows if (not up and away == 1) else group
        return remote(
            source.at[t, group], got.at[t, slot],
            z_send.at[t, int(up), away], z_recv.at[t, slot], to_row, c,
        )

    def z_got(t, slot):
        return remote(
            got.at[t, slot], got.at[t, slot],
            z_send.at[t, 0, 0], z_recv.at[t, slot], q, c,
        )

    def z_start(t, ways):
        for away in ways:
            for up in (True, False):
                @pl.when(q == (0 if up else last))
                def _():
                    z_copy(t, up, away, part).start()

    def z_pass(t):
        for away in range(last - 1, 0, -1):
            for up in (True, False):
                inside = (q > 0) & (q + away <= last) if up else (q < last) & (q - away >= 0)

                @pl.when(inside)
                def _():
                    group = q + away if up else q - away
                    z_got(t, group).wait_recv()
                    got[t, group] = got[t, group] + part[t, group]
                    z_copy(t, up, away, got).start()

    def z_wait(t):
        for away in range(1, rows):
            for up in (True, False):
                there = (q + away <= last) if up else (q - away >= 0)
                if away == 1 and t in LATE[4:6]:
                    there = there & (q != (0 if up else last))

                @pl.when(there)
                def _():
                    z_copy(t, up, away, part).wait_send()

    def near_wait(t):
        for up in (True, False):
            @pl.when(q == (0 if up else last))
            def _():
                z_copy(t, up, 1, part).wait_send()

    def strip_copy(t):
        return remote(
            part.at[t, q], matrix.at[c], s_send.at[t], s_recv.at[t], q, target[t]
        )

    def finish(t):
        @pl.when(q > 0)
        def _():
            z_got(t, q).wait_recv()
            part[t, q] = part[t, q] + got[t, q]

        @pl.when(q < last)
        def _():
            z_got(t, rows).wait_recv()
            part[t, q] = part[t, q] + got[t, rows]

        if t == 0:
            matrix[c] = part[0, q]
        else:
            strip_copy(t).start()

    def near_copy(sweep, t):
        return remote(
            r_out.at[sweep, t], r_near.at[sweep, MEET[t]],
            n_send.at[sweep, t], n_recv.at[sweep, MEET[t]], q, target[1],
        )

    def near_got(sweep, t):
        return remote(
            r_near.at[sweep, t], r_near.at[sweep, t],
            n_send.at[sweep, t], n_recv.at[sweep, t], q, target[1],
        )

    def r_copy(sweep, t):
        return remote(
            r_out.at[sweep, t], r_in.at[sweep, t],
            r_send.at[sweep, t], r_recv.at[sweep, t], q, target[t],
        )

    def out_copy(t):
        return pltpu.make_async_copy(
            pall.at[KA - 1, origin[t]], rows_ref.at[origin[t]], o_sem.at[t]
        )

    def apply_strip(sweep, t):
        if sweep == 0 and t > 0:
            strip_copy(t).wait_recv()
        r_out[sweep, t] = dot(beside(matrix[origin[t]]), x_wide[...])
        if t in MEET:
            near_copy(sweep, t).start()
        if sweep == 0:
            for group in range(rows):
                pall[KA - 1, origin[t], pl.ds(group, CB, stride=rows), :] = matrix[
                    origin[t], :, group * CB : (group + 1) * CB
                ]
            out_copy(t).start()

    def combine(sweep, t):
        near_got(sweep, t).wait_recv()
        r_out[sweep, t] = r_out[sweep, t] + r_near[sweep, t]
        if t > 0:
            r_copy(sweep, t).start()

    for t in range(KA):
        if t == 1:
            own_meta.wait()
            for copy in m_copies:
                copy.wait_recv()
            to_smem = pltpu.make_async_copy(metas, meta_s, l_sem.at[3])
            to_smem.start()
            to_smem.wait()
            p_copies[0].wait_recv()
        if t == 2:
            p_copies[1].wait_recv()
            p_copies[3].start()
            p_copies[1].wait_send()
            p_copies[2].start()
        if t == 3:
            p_copies[3].wait_recv()
        if t == 4:
            p_copies[2].wait_recv()
            p_copies[4].start()
            p_copies[2].wait_send()
            p_copies[5].start()
            p_copies[6].start()
        if t == 5:
            p_copies[4].wait_recv()
        if t == 6:
            p_copies[5].wait_recv()
            p_copies[6].wait_recv()
            p_copies[7].start()
        if t == 7:
            p_copies[7].wait_recv()
        compute(t)
        z_start(t, range(last, 0, -1) if t in LATE[:2] else range(last, 1, -1))
        if t in (4, 5):
            z_start(t - 2, [1])
        if t >= 1:
            z_pass(t - 1)
    z_start(LATE[4], [1])
    z_start(LATE[5], [1])
    z_pass(KA - 1)
    for copy in x_copies(0):
        copy.wait_recv()
    x_wide[...] = below(x_all[0].reshape(rows * CB, x_all.shape[3]))
    for i, t in enumerate(LATE):
        if i + 6 < KA:
            near_wait(LATE[i + 4])
            z_start(LATE[i + 6], [1])
        finish(t)
        if i >= 1:
            apply_strip(0, LATE[i - 1])
        if i >= 6:
            combine(0, 6 if i == 6 else 4)
    apply_strip(0, LATE[KA - 1])
    for t in (2, 0):
        combine(0, t)

    same = lax.broadcasted_iota(jnp.int32, (CB, CB), 0) == lax.broadcasted_iota(
        jnp.int32, (CB, CB), 1
    )
    diagonal = jnp.zeros((CB, 1), jnp.float32)
    for group in range(rows):
        block = matrix[c, :, group * CB : (group + 1) * CB]
        kept = jnp.where(same & (q == group), block, 0.0)
        diagonal = diagonal + jnp.sum(kept, axis=1, keepdims=True)
    scale = damping / jnp.maximum(jnp.abs(diagonal), 1.0)

    current = guess_ref[...]
    for sweep in range(2):
        if sweep == 1:
            x_all[1, q] = current
            for copy in x_copies(1):
                copy.start()
            for copy in x_copies(1):
                copy.wait_recv()
            x_wide[...] = below(x_all[1].reshape(rows * CB, x_all.shape[3]))
            for t in (7, 3, 5, 1, 6):
                apply_strip(1, t)
            combine(1, 6)
            apply_strip(1, 4)
            combine(1, 4)
            apply_strip(1, 2)
            combine(1, 2)
            apply_strip(1, 0)
            combine(1, 0)
        applied = r_out[sweep, 0]
        for t in (2, 4, 6):
            r_copy(sweep, t).wait_recv()
            applied = applied + r_in[sweep, t]
        current = current + scale * (rhs_ref[...] - applied)
    out_ref[...] = current

    for copy in p_copies + m_copies + x_copies(0) + x_copies(1):
        if copy is not p_copies[1] and copy is not p_copies[2]:
            copy.wait_send()
    for t in range(KA):
        z_wait(t)
        out_copy(t).wait()
        if t > 0:
            strip_copy(t).wait_send()
        for sweep in range(2):
            if t in MEET:
                near_copy(sweep, t).wait_send()
            elif t > 0:
                r_copy(sweep, t).wait_send()


def col_mesh(a_blocks, a_live, p_blocks, p_cols, ghost_list, policy, rates, rhs, guess):
    rows = lax.axis_size("row")
    cols = lax.axis_size("col")
    blocks = a_blocks.shape[0]
    width = rhs.shape[1]
    own_p = p_blocks.reshape(blocks, BS * KP, CB)
    vmem = pl.BlockSpec(memory_space=pltpu.VMEM)
    smem = pl.BlockSpec(memory_space=pltpu.SMEM)
    anywhere = pl.BlockSpec(memory_space=pl.ANY)
    f32, bf16 = jnp.float32, jnp.bfloat16
    dma = pltpu.SemaphoreType.DMA
    matrix, smoothed = pl.pallas_call(
        functools.partial(kernel, rows, cols),
        out_shape=(
            jax.ShapeDtypeStruct((cols, CB * rows, CB), f32),
            jax.ShapeDtypeStruct((CB, width), f32),
        ),
        in_specs=[anywhere, anywhere, vmem, vmem, smem, smem, smem, vmem, vmem, vmem],
        out_specs=(anywhere, vmem),
        scratch_shapes=[
            pltpu.VMEM((KA, blocks, BS * KP, CB), f32),
            pltpu.VMEM((cols, CB, rows * CB), f32),
            pltpu.VMEM((KA, rows, CB, rows * CB), f32),
            pltpu.VMEM((KA, rows + 1, CB, rows * CB), f32),
            pltpu.VMEM((blocks, KP * CB, 3 * BS), bf16),
            pltpu.VMEM((blocks * KP, CB, rows * CB), f32),
            pltpu.VMEM((blocks, BS, BS), f32),
            pltpu.VMEM((blocks, BS, BS), f32),
            pltpu.VMEM((2 * KA, CB), jnp.int32),
            pltpu.VMEM((cols, 2 * KA, CB), jnp.int32),
            pltpu.SMEM((cols, 2 * KA, CB), jnp.int32),
            pltpu.VMEM((2, rows, CB, width), f32),
            pltpu.VMEM((3 * rows * CB, width), bf16),
            pltpu.VMEM((2, KA, CB, width), f32),
            pltpu.VMEM((2, KA, CB, width), f32),
            pltpu.VMEM((2, KA, CB, width), f32),
            dma((2,)), dma((4,)), dma((8,)), dma((8,)), dma((cols,)), dma((cols,)),
            dma((KA, 2, rows)), dma((KA, rows + 1)), dma((KA,)), dma((KA,)),
            dma((2, rows)), dma((2, rows)), dma((2, KA)), dma((2, KA)), dma((2, KA)), dma((2, KA)), dma((KA,)),
        ],
        compiler_params=pltpu.CompilerParams(
            collective_id=0, has_side_effects=True, vmem_limit_bytes=60 * 1024 * 1024
        ),
        cost_estimate=pl.CostEstimate(
            flops=12 * KA * blocks * BS * BS * BS,
            bytes_accessed=4 * (a_blocks.size + p_blocks.size), transcendentals=0,
        ),
        name="coarse_and_sweeps",
    )(a_blocks, own_p, ghost_list, p_cols.T, p_cols.T, a_live, policy, rates, rhs, guess)
    return matrix.reshape(cols * CB, rows, 1, CB), smoothed


def on_device(a_blocks, *rest):
    blocks, slots = a_blocks.shape[:2]
    if blocks == slots == lax.axis_size("col") and lax.axis_size("row") * CB == KP * BS:
        return col_mesh(a_blocks, *rest)
    return any_mesh(a_blocks, *rest)


def solution(mesh):
    return jax.shard_map(
        on_device,
        mesh=mesh,
        in_specs=(
            P(("row", "col"), None, None, None),
            P(("row", "col"), None),
            P(("row", "col"), None, None, None),
            P(("row", "col"), None),
            P(("row", "col"), None),
            P(("row", "col")),
            P(),
            P(("row", "col"), None),
            P(("row", "col"), None),
        ),
        out_specs=(P("row", None, "col", None), P(("row", "col"), None)),
        check_vma=False,
    )
```

```python
import functools

import jax
import jax.numpy as jnp
from jax import lax
from jax.experimental import pallas as pl
from jax.experimental.pallas import tpu as pltpu
from jax.sharding import PartitionSpec as P

BS = 256
CB = 128
KA = 8
KP = 2
NPOL = 16


damping = 0.7


def from_behind(value, axis, steps):
    count = lax.axis_size(axis)
    pairs = [(source, (source + steps) % count) for source in range(count)]
    return lax.ppermute(value, axis, pairs)


def any_mesh(a_blocks, a_live, p_blocks, p_cols, ghost_list, policy, rates, rhs, guess):
    highest = lax.Precision.HIGHEST
    row_count = lax.axis_size("row")
    col_count = lax.axis_size("col")
    dev_count = row_count * col_count
    row_here = lax.axis_index("row")
    col_here = lax.axis_index("col")
    local_rows = a_blocks.shape[0]
    own_p = p_blocks.reshape(local_rows, BS, KP * CB)
    send_p = []
    send_c = []
    for offset in range(1, KA):
        picks = ghost_list[:, offset - 1]
        send_p.append(own_p[picks])
        send_c.append(p_cols[picks].astype(jnp.float32))
    incoming_p = [own_p]
    incoming_c = [p_cols]
    for offset in range(1, KA):
        moved_p, moved_c = from_behind((send_p[offset - 1], send_c[offset - 1]), "col", offset)
        incoming_p.append(moved_p)
        incoming_c.append(moved_c.astype(jnp.int32))
    ghost_p = jnp.stack(incoming_p, axis=1)
    ghost_c = jnp.stack(incoming_c, axis=1)
    live = a_live.astype(jnp.float32)
    selector = (policy[:, None] == jnp.arange(NPOL, dtype=jnp.int32)[None, :]).astype(jnp.float32)
    rate_rows = jnp.dot(selector, rates, precision=highest)
    product = jnp.einsum("skab,skbn->skan", a_blocks, ghost_p, precision=highest)
    product = product * live[:, :, None, None]
    product = product.at[:, 0].add(rate_rows[:, :, None] * own_p)
    partial_value = jnp.einsum("sam,skan->skmn", own_p, product, precision=highest)
    partial_value = (
        partial_value.reshape(local_rows, KA, KP, CB, KP, CB)
        .transpose(0, 1, 2, 4, 3, 5)
        .reshape(-1, CB, CB)
    )
    first = jnp.broadcast_to(p_cols[:, None, :, None], (local_rows, KA, KP, KP)).reshape(-1)
    second = jnp.broadcast_to(ghost_c[:, :, None, :], (local_rows, KA, KP, KP)).reshape(-1)
    alive = jnp.broadcast_to(a_live[:, :, None, None] > 0, (local_rows, KA, KP, KP)).reshape(-1)
    owner = first // col_count * col_count + second % col_count
    spot = first % col_count * row_count + second // col_count
    order = jnp.arange(owner.shape[0], dtype=jnp.int32)
    earlier = (
        (owner[None, :] == owner[:, None]) & alive[None, :] & (order[None, :] < order[:, None])
    )
    rank = jnp.sum(earlier.astype(jnp.int32), axis=1)
    row_cap = max(2, -(-(local_rows * KP) // row_count))
    slot_cap = row_cap * max(1, KA * KP // col_count)
    slot = jnp.where(alive, owner * slot_cap + rank, dev_count * slot_cap)
    sent_blocks = jax.ops.segment_sum(partial_value, slot, num_segments=dev_count * slot_cap + 1)[
        :-1
    ]
    sent_spots = jax.ops.segment_sum(
        (spot + 1).astype(jnp.float32), slot, num_segments=dev_count * slot_cap + 1
    )[:-1]
    got_blocks, got_spots = (
        lax.all_to_all(
            sent_blocks.reshape(dev_count, slot_cap, CB, CB),
            ("row", "col"),
            split_axis=0,
            concat_axis=0,
            tiled=True,
        ),
        lax.all_to_all(
            sent_spots.reshape(dev_count, slot_cap),
            ("row", "col"),
            split_axis=0,
            concat_axis=0,
            tiled=True,
        ),
    )
    places = got_spots.reshape(-1).astype(jnp.int32) - 1
    places = jnp.where(places < 0, dev_count, places)
    summed = jax.ops.segment_sum(
        got_blocks.reshape(-1, CB, CB), places, num_segments=dev_count + 1
    )[:-1]
    coarse = (
        summed.reshape(col_count, row_count, CB, CB)
        .transpose(0, 2, 1, 3)
        .reshape(col_count * CB, row_count, 1, CB)
    )
    matrix = coarse.reshape(col_count * CB, row_count * CB)
    own_block = lax.dynamic_slice(matrix, (col_here * CB, row_here * CB), (CB, CB))
    floor_diag = jnp.maximum(jnp.abs(jnp.diagonal(own_block)), 1.0)
    current = guess
    for sweep in range(2):
        gathered = lax.all_gather(current, "row", axis=0, tiled=True)
        applied = lax.psum_scatter(
            jnp.dot(matrix, gathered, precision=highest), "col", scatter_dimension=0, tiled=True
        )
        current = current + damping * (rhs - applied) / floor_diag[:, None]
    return (coarse, current)


MESH = pl.DeviceIdType.MESH
QUOT = KA
MEET = {1: 0, 3: 4, 5: 2, 7: 6}
LATE = [6, 7, 2, 3, 4, 5, 0, 1]
OPEN = 3


def halves(value):
    high = value.astype(jnp.bfloat16)
    return high, (value - high.astype(jnp.float32)).astype(jnp.bfloat16)


def beside(value):
    high, low = halves(value)
    return jnp.concatenate([high, high, low], axis=1)


def below(value):
    high, low = halves(value)
    return jnp.concatenate([high, low, high], axis=0)


def dot(left, right):
    return jnp.dot(left, right, preferred_element_type=jnp.float32)


def spread(value, names, count):
    parts = []
    for group in range(count):
        part = 0.0
        for m, name in enumerate(names):
            part = part + jnp.where(name == group, value[:, m * CB : (m + 1) * CB], 0.0)
        parts.append(part)
    return jnp.concatenate(parts, axis=1)


def kernel(
    rows, cols, a_ref, p_ref, taken_ref, cols_ref, own_ref, live_ref, policy_ref, rate_ref,
    rhs_ref, guess_ref,
    matrix, out_ref,
    pall, part, got, ecat, products, abuf0, abuf1, meta_ref, metas, meta_s, x_all, x_wide, r_out, r_near, r_in,
    a_sem, l_sem, p_send, p_recv, m_send, m_recv, z_send, z_recv, s_send, s_recv,
    x_send, x_recv, r_send, r_recv, n_send, n_recv,
):
    q = lax.axis_index("row")
    c = lax.axis_index("col")
    last = rows - 1
    blocks = pall.shape[1]
    digit_y, digit_x, core = c // 4, (c // 2) % 2, c % 2
    other = 1 - core
    swap_y, swap_x, swap_c = 1 - 2 * digit_y, 1 - 2 * digit_x, 1 - 2 * core

    def peer(flips):
        return c + flips[0] * swap_y * 4 + flips[1] * swap_x * 2 + flips[2] * swap_c

    to_flips = [
        (0, 0, 0), (0, 0, 1), (core, other, 0), (other, core, 1),
        (other, core, 0), (core, other, 1), (1, 1, 0), (1, 1, 1),
    ]
    from_flips = list(to_flips)
    from_flips[3], from_flips[5] = to_flips[5], to_flips[3]
    target = [peer(flips) for flips in to_flips]
    origin = [peer(flips) for flips in from_flips]
    plain = [peer((f // 4, (f // 2) % 2, f % 2)) for f in range(cols)]
    slot_k = [lax.rem(c - e + cols, cols) for e in target]
    abufs = [abuf0, abuf1]

    def remote(src, dst, send, recv, row, col):
        return pltpu.make_async_remote_copy(
            src_ref=src, dst_ref=dst, send_sem=send, recv_sem=recv,
            device_id=(row, col), device_id_type=MESH,
        )

    def load_a(t):
        return pltpu.make_async_copy(
            a_ref.at[:, slot_k[t]], abufs[t % 2], a_sem.at[t % 2]
        )

    own_p = pltpu.make_async_copy(p_ref, pall.at[0], l_sem.at[0])
    own_p.start()
    load_a(0).start()
    meta_ref[...] = jnp.zeros_like(meta_ref)
    meta_ref[0:blocks, 0 : KA - 1] = taken_ref[...]
    meta_ref[QUOT : QUOT + KP, 0:blocks] = cols_ref[...]
    own_meta = pltpu.make_async_copy(meta_ref, metas.at[c], l_sem.at[1])
    own_meta.start()
    own_x = pltpu.make_async_copy(guess_ref, x_all.at[0, q], l_sem.at[2])
    own_x.start()

    barrier = pltpu.get_barrier_semaphore()
    for f in range(1, cols):
        pl.semaphore_signal(barrier, inc=1, device_id=(q, plain[f]), device_id_type=MESH)
    row_peer = [lax.rem(q + step, rows) for step in range(rows)]
    for step in range(1, rows):
        pl.semaphore_signal(barrier, inc=1, device_id=(row_peer[step], c), device_id_type=MESH)
    pl.semaphore_wait(barrier, cols - 1 + rows - 1)

    mid = blocks // 2
    p_copies = [
        remote(p_ref, pall.at[1], p_send.at[0], p_recv.at[0], q, target[1]),
        remote(p_ref, pall.at[2], p_send.at[1], p_recv.at[1], q, target[2]),
        remote(p_ref, pall.at[4], p_send.at[2], p_recv.at[2], q, target[4]),
        remote(pall.at[2], pall.at[3], p_send.at[3], p_recv.at[3], q, target[1]),
        remote(pall.at[4], pall.at[5], p_send.at[4], p_recv.at[4], q, target[1]),
        remote(
            pall.at[4, pl.ds(0, mid)], pall.at[6, pl.ds(0, mid)],
            p_send.at[5], p_recv.at[5], q, target[2],
        ),
        remote(
            pall.at[2, pl.ds(mid, blocks - mid)], pall.at[6, pl.ds(mid, blocks - mid)],
            p_send.at[6], p_recv.at[6], q, target[4],
        ),
        remote(pall.at[6], pall.at[7], p_send.at[7], p_recv.at[7], q, target[1]),
    ]
    m_copies = [
        remote(meta_ref, metas.at[c], m_send.at[f], m_recv.at[f], q, plain[f])
        for f in range(1, cols)
    ]

    p_copies[0].start()
    p_copies[1].start()
    for copy in m_copies:
        copy.start()
    own_x.wait()

    def x_copies(sweep):
        return [
            remote(
                x_all.at[sweep, q], x_all.at[sweep, q],
                x_send.at[sweep, step], x_recv.at[sweep, step], row_peer[step], c,
            )
            for step in range(1, rows)
        ]

    for copy in x_copies(0):
        copy.start()
    own_p.wait()

    own_names = [[lax.div(own_ref[m, j], cols) for m in range(KP)] for j in range(blocks)]
    places = []
    for group in range(rows):
        found = 0
        slots = [(0, 0)] * (blocks * KP // rows)
        for j in range(blocks):
            for m in range(KP):
                hit = own_names[j][m] == group
                slots = [
                    (
                        jnp.where(hit & (found == rank), j, held[0]),
                        jnp.where(hit & (found == rank), m, held[1]),
                    )
                    for rank, held in enumerate(slots)
                ]
                found = found + hit.astype(jnp.int32)
        places.append(slots)

    def p_block(t, j):
        return jnp.concatenate(
            [pall[t, j, pl.ds(m, BS, stride=KP), :] for m in range(KP)], axis=1
        )

    eye = lax.broadcasted_iota(jnp.int32, (BS, BS), 0) == lax.broadcasted_iota(
        jnp.int32, (BS, BS), 1
    )

    def compute(t):
        load_a(t).wait()
        if t + 1 < KA:
            load_a(t + 1).start()
        abuf = abufs[t % 2]

        def one(j, _):
            if t == 0:
                s = j
                ecat[j] = beside(p_block(0, j).T)
                names = [lax.div(own_ref[m, j], cols) for m in range(KP)]
            else:
                s = 0
                for held in range(blocks):
                    taken = meta_s[target[t], held, slot_k[t] - 1]
                    s = jnp.where(taken == j, held, s)
                names = [lax.div(meta_s[target[t], QUOT + m, j], cols) for m in range(KP)]
            block = abuf[s] * live_ref[s, slot_k[t]].astype(jnp.float32)
            if t == 0:
                block = block + jnp.where(eye, rate_ref[pl.ds(policy_ref[j], 1), :], 0.0)
            product = dot(beside(block), below(p_block(t, j)))
            product = spread(dot(ecat[s], below(product)), names, rows)
            for m in range(KP):
                products[KP * j + m] = product[m * CB : (m + 1) * CB]
            return 0

        lax.fori_loop(0, blocks, one, 0)
        for group in range(rows):
            total = None
            for s, m in places[group]:
                j = s if t == 0 else meta_s[target[t], s, slot_k[t] - 1]
                one_of = products[KP * j + m]
                total = one_of if total is None else total + one_of
            part[t, group] = total

    def z_copy(t, up, away, source):
        group = q + away if up else q - away
        to_row = q + 1 if up else q - 1
        slot = rows if (not up and away == 1) else group
        return remote(
            source.at[t, group], got.at[t, slot],
            z_send.at[t, int(up), away], z_recv.at[t, slot], to_row, c,
        )

    def z_got(t, slot):
        return remote(
            got.at[t, slot], got.at[t, slot],
            z_send.at[t, 0, 0], z_recv.at[t, slot], q, c,
        )

    def z_start(t, ways):
        for away in ways:
            for up in (True, False):
                @pl.when(q == (0 if up else last))
                def _():
                    z_copy(t, up, away, part).start()

    def z_pass(t):
        for away in range(last - 1, 0, -1):
            for up in (True, False):
                inside = (q > 0) & (q + away <= last) if up else (q < last) & (q - away >= 0)

                @pl.when(inside)
                def _():
                    group = q + away if up else q - away
                    z_got(t, group).wait_recv()
                    got[t, group] = got[t, group] + part[t, group]
                    z_copy(t, up, away, got).start()

    def z_wait(t):
        for away in range(1, rows):
            for up in (True, False):
                there = (q + away <= last) if up else (q - away >= 0)
                if t in LATE[:2] or (away == 1 and t in LATE[: KA - OPEN]):
                    there = there & (q != (0 if up else last))

                @pl.when(there)
                def _():
                    z_copy(t, up, away, part).wait_send()

    def sent(t, ways):
        for up in (True, False):
            @pl.when(q == (0 if up else last))
            def _():
                for away in ways:
                    z_copy(t, up, away, part).wait_send()

    def strip_copy(t):
        return remote(
            part.at[t, q], matrix.at[c], s_send.at[t], s_recv.at[t], q, target[t]
        )

    def finish(t):
        @pl.when(q > 0)
        def _():
            z_got(t, q).wait_recv()
            part[t, q] = part[t, q] + got[t, q]

        @pl.when(q < last)
        def _():
            z_got(t, rows).wait_recv()
            part[t, q] = part[t, q] + got[t, rows]

        if t == 0:
            matrix[c] = part[0, q]
        else:
            strip_copy(t).start()

    def near_copy(sweep, t):
        return remote(
            r_out.at[sweep, t], r_near.at[sweep, MEET[t]],
            n_send.at[sweep, t], n_recv.at[sweep, MEET[t]], q, target[1],
        )

    def near_got(sweep, t):
        return remote(
            r_near.at[sweep, t], r_near.at[sweep, t],
            n_send.at[sweep, t], n_recv.at[sweep, t], q, target[1],
        )

    def r_copy(sweep, t):
        return remote(
            r_out.at[sweep, t], r_in.at[sweep, t],
            r_send.at[sweep, t], r_recv.at[sweep, t], q, target[t],
        )

    def apply_strip(t):
        if t > 0:
            strip_copy(t).wait_recv()
        r_out[0, t] = dot(beside(matrix[origin[t]]), x_wide[...])
        if t in MEET:
            near_copy(0, t).start()

    def combine(sweep, t):
        near_got(sweep, t).wait_recv()
        r_out[sweep, t] = r_out[sweep, t] + r_near[sweep, t]
        if t > 0:
            r_copy(sweep, t).start()

    for t in range(KA):
        if t == 1:
            own_meta.wait()
            for copy in m_copies:
                copy.wait_recv()
            to_smem = pltpu.make_async_copy(metas, meta_s, l_sem.at[3])
            to_smem.start()
            to_smem.wait()
            p_copies[0].wait_recv()
        if t == 2:
            p_copies[1].wait_recv()
            p_copies[3].start()
            p_copies[1].wait_send()
            p_copies[2].start()
        if t == 3:
            p_copies[3].wait_recv()
        if t == 4:
            p_copies[2].wait_recv()
            p_copies[4].start()
            p_copies[2].wait_send()
            p_copies[5].start()
            p_copies[6].start()
        if t == 5:
            p_copies[4].wait_recv()
        if t == 6:
            p_copies[5].wait_recv()
            p_copies[6].wait_recv()
            p_copies[7].start()
        if t == 7:
            p_copies[7].wait_recv()
        compute(t)
        z_start(t, range(last, 1, -1))
        if t >= 1:
            z_pass(t - 1)
    sent(LATE[0], range(last, 1, -1))
    z_start(LATE[0], [1])
    sent(LATE[1], range(last, 1, -1))
    for t in LATE[1:OPEN]:
        z_start(t, [1])
    z_pass(KA - 1)
    for copy in x_copies(0):
        copy.wait_recv()
    x_wide[...] = below(x_all[0].reshape(rows * CB, x_all.shape[3]))
    for i, t in enumerate(LATE):
        if i + OPEN < KA:
            sent(t, [1])
            z_start(LATE[i + OPEN], [1])
        finish(t)
        if i >= 1:
            apply_strip(LATE[i - 1])
        if i in (4, 6, 7):
            combine(0, {4: 6, 6: 4, 7: 2}[i])
    apply_strip(LATE[KA - 1])
    combine(0, 0)

    same = lax.broadcasted_iota(jnp.int32, (CB, CB), 0) == lax.broadcasted_iota(
        jnp.int32, (CB, CB), 1
    )
    diagonal = jnp.zeros((CB, 1), jnp.float32)
    for group in range(rows):
        block = matrix[c, :, group * CB : (group + 1) * CB]
        kept = jnp.where(same & (q == group), block, 0.0)
        diagonal = diagonal + jnp.sum(kept, axis=1, keepdims=True)
    scale = damping / jnp.maximum(jnp.abs(diagonal), 1.0)

    current = guess_ref[...]
    for sweep in range(2):
        if sweep == 1:
            x_all[1, q] = current
            for copy in x_copies(1):
                copy.start()
            copies = x_copies(1)
            for step in range(rows):
                if step > 0:
                    copies[step - 1].wait_recv()
                group = lax.rem(q + rows - step, rows)
                x_part = below(x_all[1, group])
                lanes = pl.ds(pl.multiple_of(group * CB, CB), CB)
                for t in (7, 3, 5, 1, 6, 4, 2, 0):
                    more = dot(beside(matrix[origin[t], :, lanes]), x_part)
                    r_out[1, t] = more if step == 0 else r_out[1, t] + more
                    if step == last and t in MEET:
                        near_copy(1, t).start()
                    elif step == last:
                        combine(1, t)
        applied = r_out[sweep, 0]
        for t in (2, 4, 6):
            r_copy(sweep, t).wait_recv()
            applied = applied + r_in[sweep, t]
        current = current + scale * (rhs_ref[...] - applied)
    out_ref[...] = current

    for copy in p_copies + m_copies + x_copies(0) + x_copies(1):
        if copy is not p_copies[1] and copy is not p_copies[2]:
            copy.wait_send()
    for t in range(KA):
        z_wait(t)
        if t > 0:
            strip_copy(t).wait_send()
        for sweep in range(2):
            if t in MEET:
                near_copy(sweep, t).wait_send()
            elif t > 0:
                r_copy(sweep, t).wait_send()


def col_mesh(a_blocks, a_live, p_blocks, p_cols, ghost_list, policy, rates, rhs, guess):
    rows = lax.axis_size("row")
    cols = lax.axis_size("col")
    blocks = a_blocks.shape[0]
    width = rhs.shape[1]
    own_p = p_blocks.reshape(blocks, BS * KP, CB)
    vmem = pl.BlockSpec(memory_space=pltpu.VMEM)
    smem = pl.BlockSpec(memory_space=pltpu.SMEM)
    anywhere = pl.BlockSpec(memory_space=pl.ANY)
    f32, bf16 = jnp.float32, jnp.bfloat16
    dma = pltpu.SemaphoreType.DMA
    matrix, smoothed = pl.pallas_call(
        functools.partial(kernel, rows, cols),
        out_shape=(
            jax.ShapeDtypeStruct((cols, CB, rows * CB), f32),
            jax.ShapeDtypeStruct((CB, width), f32),
        ),
        in_specs=[anywhere, anywhere, vmem, vmem, smem, smem, smem, vmem, vmem, vmem],
        out_specs=(vmem, vmem),
        scratch_shapes=[
            pltpu.VMEM((KA, blocks, BS * KP, CB), f32),
            pltpu.VMEM((KA, rows, CB, rows * CB), f32),
            pltpu.VMEM((KA, rows + 1, CB, rows * CB), f32),
            pltpu.VMEM((blocks, KP * CB, 3 * BS), bf16),
            pltpu.VMEM((blocks * KP, CB, rows * CB), f32),
            pltpu.VMEM((blocks, BS, BS), f32),
            pltpu.VMEM((blocks, BS, BS), f32),
            pltpu.VMEM((2 * KA, CB), jnp.int32),
            pltpu.VMEM((cols, 2 * KA, CB), jnp.int32),
            pltpu.SMEM((cols, 2 * KA, CB), jnp.int32),
            pltpu.VMEM((2, rows, CB, width), f32),
            pltpu.VMEM((3 * rows * CB, width), bf16),
            pltpu.VMEM((2, KA, CB, width), f32),
            pltpu.VMEM((2, KA, CB, width), f32),
            pltpu.VMEM((2, KA, CB, width), f32),
            dma((2,)), dma((4,)), dma((8,)), dma((8,)), dma((cols,)), dma((cols,)),
            dma((KA, 2, rows)), dma((KA, rows + 1)), dma((KA,)), dma((KA,)),
            dma((2, rows)), dma((2, rows)), dma((2, KA)), dma((2, KA)), dma((2, KA)), dma((2, KA)),
        ],
        compiler_params=pltpu.CompilerParams(
            collective_id=0, has_side_effects=True, vmem_limit_bytes=60 * 1024 * 1024
        ),
        cost_estimate=pl.CostEstimate(
            flops=12 * KA * blocks * BS * BS * BS,
            bytes_accessed=4 * (a_blocks.size + p_blocks.size), transcendentals=0,
        ),
        name="coarse_and_sweeps",
    )(a_blocks, own_p, ghost_list, p_cols.T, p_cols.T, a_live, policy, rates, rhs, guess)
    return matrix.reshape(cols * CB, rows, 1, CB), smoothed


def on_device(a_blocks, *rest):
    blocks, slots = a_blocks.shape[:2]
    if blocks == slots == lax.axis_size("col") and lax.axis_size("row") * CB == KP * BS:
        return col_mesh(a_blocks, *rest)
    return any_mesh(a_blocks, *rest)


def solution(mesh):
    return jax.shard_map(
        on_device,
        mesh=mesh,
        in_specs=(
            P(("row", "col"), None, None, None),
            P(("row", "col"), None),
            P(("row", "col"), None, None, None),
            P(("row", "col"), None),
            P(("row", "col"), None),
            P(("row", "col")),
            P(),
            P(("row", "col"), None),
            P(("row", "col"), None),
        ),
        out_specs=(P("row", None, "col", None), P(("row", "col"), None)),
        check_vma=False,
    )
```

```python
import functools

import jax
import jax.numpy as jnp
from jax import lax
from jax.experimental import pallas as pl
from jax.experimental.pallas import tpu as pltpu
from jax.sharding import PartitionSpec as P

BS = 256
CB = 128
KA = 8
KP = 2
NPOL = 16


damping = 0.7


def from_behind(value, axis, steps):
    count = lax.axis_size(axis)
    pairs = [(source, (source + steps) % count) for source in range(count)]
    return lax.ppermute(value, axis, pairs)


def any_mesh(a_blocks, a_live, p_blocks, p_cols, ghost_list, policy, rates, rhs, guess):
    highest = lax.Precision.HIGHEST
    row_count = lax.axis_size("row")
    col_count = lax.axis_size("col")
    dev_count = row_count * col_count
    row_here = lax.axis_index("row")
    col_here = lax.axis_index("col")
    local_rows = a_blocks.shape[0]
    own_p = p_blocks.reshape(local_rows, BS, KP * CB)
    send_p = []
    send_c = []
    for offset in range(1, KA):
        picks = ghost_list[:, offset - 1]
        send_p.append(own_p[picks])
        send_c.append(p_cols[picks].astype(jnp.float32))
    incoming_p = [own_p]
    incoming_c = [p_cols]
    for offset in range(1, KA):
        moved_p, moved_c = from_behind((send_p[offset - 1], send_c[offset - 1]), "col", offset)
        incoming_p.append(moved_p)
        incoming_c.append(moved_c.astype(jnp.int32))
    ghost_p = jnp.stack(incoming_p, axis=1)
    ghost_c = jnp.stack(incoming_c, axis=1)
    live = a_live.astype(jnp.float32)
    selector = (policy[:, None] == jnp.arange(NPOL, dtype=jnp.int32)[None, :]).astype(jnp.float32)
    rate_rows = jnp.dot(selector, rates, precision=highest)
    product = jnp.einsum("skab,skbn->skan", a_blocks, ghost_p, precision=highest)
    product = product * live[:, :, None, None]
    product = product.at[:, 0].add(rate_rows[:, :, None] * own_p)
    partial_value = jnp.einsum("sam,skan->skmn", own_p, product, precision=highest)
    partial_value = (
        partial_value.reshape(local_rows, KA, KP, CB, KP, CB)
        .transpose(0, 1, 2, 4, 3, 5)
        .reshape(-1, CB, CB)
    )
    first = jnp.broadcast_to(p_cols[:, None, :, None], (local_rows, KA, KP, KP)).reshape(-1)
    second = jnp.broadcast_to(ghost_c[:, :, None, :], (local_rows, KA, KP, KP)).reshape(-1)
    alive = jnp.broadcast_to(a_live[:, :, None, None] > 0, (local_rows, KA, KP, KP)).reshape(-1)
    owner = first // col_count * col_count + second % col_count
    spot = first % col_count * row_count + second // col_count
    order = jnp.arange(owner.shape[0], dtype=jnp.int32)
    earlier = (
        (owner[None, :] == owner[:, None]) & alive[None, :] & (order[None, :] < order[:, None])
    )
    rank = jnp.sum(earlier.astype(jnp.int32), axis=1)
    row_cap = max(2, -(-(local_rows * KP) // row_count))
    slot_cap = row_cap * max(1, KA * KP // col_count)
    slot = jnp.where(alive, owner * slot_cap + rank, dev_count * slot_cap)
    sent_blocks = jax.ops.segment_sum(partial_value, slot, num_segments=dev_count * slot_cap + 1)[
        :-1
    ]
    sent_spots = jax.ops.segment_sum(
        (spot + 1).astype(jnp.float32), slot, num_segments=dev_count * slot_cap + 1
    )[:-1]
    got_blocks, got_spots = (
        lax.all_to_all(
            sent_blocks.reshape(dev_count, slot_cap, CB, CB),
            ("row", "col"),
            split_axis=0,
            concat_axis=0,
            tiled=True,
        ),
        lax.all_to_all(
            sent_spots.reshape(dev_count, slot_cap),
            ("row", "col"),
            split_axis=0,
            concat_axis=0,
            tiled=True,
        ),
    )
    places = got_spots.reshape(-1).astype(jnp.int32) - 1
    places = jnp.where(places < 0, dev_count, places)
    summed = jax.ops.segment_sum(
        got_blocks.reshape(-1, CB, CB), places, num_segments=dev_count + 1
    )[:-1]
    coarse = (
        summed.reshape(col_count, row_count, CB, CB)
        .transpose(0, 2, 1, 3)
        .reshape(col_count * CB, row_count, 1, CB)
    )
    matrix = coarse.reshape(col_count * CB, row_count * CB)
    own_block = lax.dynamic_slice(matrix, (col_here * CB, row_here * CB), (CB, CB))
    floor_diag = jnp.maximum(jnp.abs(jnp.diagonal(own_block)), 1.0)
    current = guess
    for sweep in range(2):
        gathered = lax.all_gather(current, "row", axis=0, tiled=True)
        applied = lax.psum_scatter(
            jnp.dot(matrix, gathered, precision=highest), "col", scatter_dimension=0, tiled=True
        )
        current = current + damping * (rhs - applied) / floor_diag[:, None]
    return (coarse, current)


MESH = pl.DeviceIdType.MESH
QUOT = KA
MEET = {1: 0, 3: 4, 5: 2, 7: 6}
LATE = [6, 7, 2, 3, 4, 5, 0, 1]
OPEN = 3


def halves(value):
    high = value.astype(jnp.bfloat16)
    return high, (value - high.astype(jnp.float32)).astype(jnp.bfloat16)


def beside(value):
    high, low = halves(value)
    return jnp.concatenate([high, high, low], axis=1)


def below(value):
    high, low = halves(value)
    return jnp.concatenate([high, low, high], axis=0)


def dot(left, right):
    return jnp.dot(left, right, preferred_element_type=jnp.float32)


def spread(value, names, count):
    parts = []
    for group in range(count):
        part = 0.0
        for m, name in enumerate(names):
            part = part + jnp.where(name == group, value[:, m * CB : (m + 1) * CB], 0.0)
        parts.append(part)
    return jnp.concatenate(parts, axis=1)


def kernel(
    rows, cols, a_ref, p_ref, taken_ref, cols_ref, own_ref, live_ref, policy_ref, rate_ref,
    rhs_ref, guess_ref,
    matrix, out_ref,
    pall, part, got, ecat, products, abuf0, abuf1, meta_ref, metas, meta_s, x_all, x_wide, r_out, r_near, r_in,
    a_sem, l_sem, p_send, p_recv, m_send, m_recv, z_send, z_recv, s_send, s_recv,
    x_send, x_recv, r_send, r_recv, n_send, n_recv,
):
    q = lax.axis_index("row")
    c = lax.axis_index("col")
    last = rows - 1
    blocks = pall.shape[1]
    digit_y, digit_x, core = c // 4, (c // 2) % 2, c % 2
    other = 1 - core
    swap_y, swap_x, swap_c = 1 - 2 * digit_y, 1 - 2 * digit_x, 1 - 2 * core

    def peer(flips):
        return c + flips[0] * swap_y * 4 + flips[1] * swap_x * 2 + flips[2] * swap_c

    to_flips = [
        (0, 0, 0), (0, 0, 1), (core, other, 0), (other, core, 1),
        (other, core, 0), (core, other, 1), (1, 1, 0), (1, 1, 1),
    ]
    from_flips = list(to_flips)
    from_flips[3], from_flips[5] = to_flips[5], to_flips[3]
    target = [peer(flips) for flips in to_flips]
    origin = [peer(flips) for flips in from_flips]
    plain = [peer((f // 4, (f // 2) % 2, f % 2)) for f in range(cols)]
    slot_k = [lax.rem(c - e + cols, cols) for e in target]
    abufs = [abuf0, abuf1]

    def remote(src, dst, send, recv, row, col):
        return pltpu.make_async_remote_copy(
            src_ref=src, dst_ref=dst, send_sem=send, recv_sem=recv,
            device_id=(row, col), device_id_type=MESH,
        )

    def load_a(t):
        return pltpu.make_async_copy(
            a_ref.at[:, slot_k[t]], abufs[t % 2], a_sem.at[t % 2]
        )

    own_p = pltpu.make_async_copy(p_ref, pall.at[0], l_sem.at[0])
    own_p.start()
    load_a(0).start()
    meta_ref[...] = jnp.zeros_like(meta_ref)
    meta_ref[0:blocks, 0 : KA - 1] = taken_ref[...]
    meta_ref[QUOT : QUOT + KP, 0:blocks] = cols_ref[...]
    own_meta = pltpu.make_async_copy(meta_ref, metas.at[c], l_sem.at[1])
    own_meta.start()
    own_x = pltpu.make_async_copy(guess_ref, x_all.at[0, q], l_sem.at[2])
    own_x.start()

    barrier = pltpu.get_barrier_semaphore()
    for f in range(1, cols):
        pl.semaphore_signal(barrier, inc=1, device_id=(q, plain[f]), device_id_type=MESH)
    row_peer = [lax.rem(q + step, rows) for step in range(rows)]
    for step in range(1, rows):
        pl.semaphore_signal(barrier, inc=1, device_id=(row_peer[step], c), device_id_type=MESH)
    pl.semaphore_wait(barrier, cols - 1 + rows - 1)

    mid = blocks // 2
    p_copies = [
        remote(p_ref, pall.at[1], p_send.at[0], p_recv.at[0], q, target[1]),
        remote(p_ref, pall.at[2], p_send.at[1], p_recv.at[1], q, target[2]),
        remote(p_ref, pall.at[4], p_send.at[2], p_recv.at[2], q, target[4]),
        remote(pall.at[2], pall.at[3], p_send.at[3], p_recv.at[3], q, target[1]),
        remote(pall.at[4], pall.at[5], p_send.at[4], p_recv.at[4], q, target[1]),
        remote(
            pall.at[4, pl.ds(0, mid)], pall.at[6, pl.ds(0, mid)],
            p_send.at[5], p_recv.at[5], q, target[2],
        ),
        remote(
            pall.at[2, pl.ds(mid, blocks - mid)], pall.at[6, pl.ds(mid, blocks - mid)],
            p_send.at[6], p_recv.at[6], q, target[4],
        ),
        remote(pall.at[6], pall.at[7], p_send.at[7], p_recv.at[7], q, target[1]),
    ]
    m_copies = [
        remote(meta_ref, metas.at[c], m_send.at[f], m_recv.at[f], q, plain[f])
        for f in range(1, cols)
    ]

    p_copies[0].start()
    p_copies[1].start()
    for copy in m_copies:
        copy.start()
    own_x.wait()

    def x_copies(sweep):
        return [
            remote(
                x_all.at[sweep, q], x_all.at[sweep, q],
                x_send.at[sweep, step], x_recv.at[sweep, step], row_peer[step], c,
            )
            for step in range(1, rows)
        ]

    for copy in x_copies(0):
        copy.start()
    own_p.wait()

    own_names = [[lax.div(own_ref[m, j], cols) for m in range(KP)] for j in range(blocks)]
    places = []
    for group in range(rows):
        found = 0
        slots = [(0, 0)] * (blocks * KP // rows)
        for j in range(blocks):
            for m in range(KP):
                hit = own_names[j][m] == group
                slots = [
                    (
                        jnp.where(hit & (found == rank), j, held[0]),
                        jnp.where(hit & (found == rank), m, held[1]),
                    )
                    for rank, held in enumerate(slots)
                ]
                found = found + hit.astype(jnp.int32)
        places.append(slots)

    def p_block(t, j):
        return jnp.concatenate(
            [pall[t, j, pl.ds(m, BS, stride=KP), :] for m in range(KP)], axis=1
        )

    eye = lax.broadcasted_iota(jnp.int32, (BS, BS), 0) == lax.broadcasted_iota(
        jnp.int32, (BS, BS), 1
    )

    def compute(t):
        load_a(t).wait()
        if t + 1 < KA:
            load_a(t + 1).start()
        abuf = abufs[t % 2]

        def one(j, _):
            if t == 0:
                s = j
                ecat[j] = beside(p_block(0, j).T)
                names = [lax.div(own_ref[m, j], cols) for m in range(KP)]
            else:
                s = 0
                for held in range(blocks):
                    taken = meta_s[target[t], held, slot_k[t] - 1]
                    s = jnp.where(taken == j, held, s)
                names = [lax.div(meta_s[target[t], QUOT + m, j], cols) for m in range(KP)]
            block = abuf[s] * live_ref[s, slot_k[t]].astype(jnp.float32)
            if t == 0:
                block = block + jnp.where(eye, rate_ref[pl.ds(policy_ref[j], 1), :], 0.0)
            product = dot(beside(block), below(p_block(t, j)))
            product = spread(dot(ecat[s], below(product)), names, rows)
            for m in range(KP):
                products[KP * j + m] = product[m * CB : (m + 1) * CB]
            return 0

        lax.fori_loop(0, blocks, one, 0)
        for group in range(rows):
            total = None
            for s, m in places[group]:
                j = s if t == 0 else meta_s[target[t], s, slot_k[t] - 1]
                one_of = products[KP * j + m]
                total = one_of if total is None else total + one_of
            part[t, group] = total

    def z_copy(t, up, away, source):
        group = q + away if up else q - away
        to_row = q + 1 if up else q - 1
        slot = rows if (not up and away == 1) else group
        return remote(
            source.at[t, group], got.at[t, slot],
            z_send.at[t, int(up), away], z_recv.at[t, slot], to_row, c,
        )

    def z_got(t, slot):
        return remote(
            got.at[t, slot], got.at[t, slot],
            z_send.at[t, 0, 0], z_recv.at[t, slot], q, c,
        )

    def z_start(t, ways):
        for away in ways:
            for up in (True, False):
                @pl.when(q == (0 if up else last))
                def _():
                    z_copy(t, up, away, part).start()

    def z_pass(t):
        for away in range(last - 1, 0, -1):
            for up in (True, False):
                inside = (q > 0) & (q + away <= last) if up else (q < last) & (q - away >= 0)

                @pl.when(inside)
                def _():
                    group = q + away if up else q - away
                    z_got(t, group).wait_recv()
                    got[t, group] = got[t, group] + part[t, group]
                    z_copy(t, up, away, got).start()

    def z_wait(t):
        for away in range(1, rows):
            for up in (True, False):
                there = (q + away <= last) if up else (q - away >= 0)
                if t in LATE[:2] or (away == 1 and t in LATE[: KA - OPEN]):
                    there = there & (q != (0 if up else last))

                @pl.when(there)
                def _():
                    z_copy(t, up, away, part).wait_send()

    def sent(t, ways):
        for up in (True, False):
            @pl.when(q == (0 if up else last))
            def _():
                for away in ways:
                    z_copy(t, up, away, part).wait_send()

    def strip_copy(t):
        return remote(
            part.at[t, q], matrix.at[c], s_send.at[t], s_recv.at[t], q, target[t]
        )

    def finish(t):
        @pl.when(q > 0)
        def _():
            z_got(t, q).wait_recv()
            part[t, q] = part[t, q] + got[t, q]

        @pl.when(q < last)
        def _():
            z_got(t, rows).wait_recv()
            part[t, q] = part[t, q] + got[t, rows]

        if t == 0:
            matrix[c] = part[0, q]
        else:
            strip_copy(t).start()

    def near_copy(sweep, t):
        return remote(
            r_out.at[sweep, t], r_near.at[sweep, MEET[t]],
            n_send.at[sweep, t], n_recv.at[sweep, MEET[t]], q, target[1],
        )

    def near_got(sweep, t):
        return remote(
            r_near.at[sweep, t], r_near.at[sweep, t],
            n_send.at[sweep, t], n_recv.at[sweep, t], q, target[1],
        )

    def r_copy(sweep, t):
        return remote(
            r_out.at[sweep, t], r_in.at[sweep, t],
            r_send.at[sweep, t], r_recv.at[sweep, t], q, target[t],
        )

    def apply_strip(t):
        if t > 0:
            strip_copy(t).wait_recv()
        r_out[0, t] = dot(beside(matrix[origin[t]]), x_wide[...])
        if t in MEET:
            near_copy(0, t).start()

    def combine(sweep, t):
        near_got(sweep, t).wait_recv()
        r_out[sweep, t] = r_out[sweep, t] + r_near[sweep, t]
        if t > 0:
            r_copy(sweep, t).start()

    def row_scale():
        same = lax.broadcasted_iota(jnp.int32, (CB, CB), 0) == lax.broadcasted_iota(
            jnp.int32, (CB, CB), 1
        )
        diagonal = jnp.zeros((CB, 1), jnp.float32)
        for group in range(rows):
            block = matrix[c, :, group * CB : (group + 1) * CB]
            kept = jnp.where(same & (q == group), block, 0.0)
            diagonal = diagonal + jnp.sum(kept, axis=1, keepdims=True)
        return damping / jnp.maximum(jnp.abs(diagonal), 1.0)

    for t in range(KA):
        if t == 1:
            own_meta.wait()
            for copy in m_copies:
                copy.wait_recv()
            to_smem = pltpu.make_async_copy(metas, meta_s, l_sem.at[3])
            to_smem.start()
            to_smem.wait()
            p_copies[0].wait_recv()
        if t == 2:
            p_copies[1].wait_recv()
            p_copies[3].start()
            p_copies[1].wait_send()
            p_copies[2].start()
        if t == 3:
            p_copies[3].wait_recv()
        if t == 4:
            p_copies[2].wait_recv()
            p_copies[4].start()
            p_copies[2].wait_send()
            p_copies[5].start()
            p_copies[6].start()
        if t == 5:
            p_copies[4].wait_recv()
        if t == 6:
            p_copies[5].wait_recv()
            p_copies[6].wait_recv()
            p_copies[7].start()
        if t == 7:
            p_copies[7].wait_recv()
        compute(t)
        z_start(t, range(last, 1, -1))
        if t >= 1:
            z_pass(t - 1)
    sent(LATE[0], range(last, 1, -1))
    z_start(LATE[0], [1])
    sent(LATE[1], range(last, 1, -1))
    for t in LATE[1:OPEN]:
        z_start(t, [1])
    z_pass(KA - 1)
    for copy in x_copies(0):
        copy.wait_recv()
    x_wide[...] = below(x_all[0].reshape(rows * CB, x_all.shape[3]))
    for i, t in enumerate(LATE):
        if i + OPEN < KA:
            sent(t, [1])
            z_start(LATE[i + OPEN], [1])
        if i >= 1:
            apply_strip(LATE[i - 1])
        if i in (3, 6, 7):
            combine(0, {3: 6, 6: 4, 7: 2}[i])
        if i == KA - 1:
            scale = row_scale()
        finish(t)
    apply_strip(LATE[KA - 1])
    combine(0, 0)

    current = guess_ref[...]
    for sweep in range(2):
        if sweep == 1:
            x_all[1, q] = current
            for copy in x_copies(1):
                copy.start()
            copies = x_copies(1)
            for step in range(rows):
                if step > 0:
                    copies[step - 1].wait_recv()
                group = lax.rem(q + rows - step, rows)
                x_part = below(x_all[1, group])
                lanes = pl.ds(pl.multiple_of(group * CB, CB), CB)
                for t in (7, 3, 5, 1, 6, 4, 2, 0):
                    more = dot(beside(matrix[origin[t], :, lanes]), x_part)
                    r_out[1, t] = more if step == 0 else r_out[1, t] + more
                    if step == last and t in MEET:
                        near_copy(1, t).start()
                    elif step == last:
                        combine(1, t)
        applied = r_out[sweep, 0]
        for t in (2, 4, 6):
            r_copy(sweep, t).wait_recv()
            applied = applied + r_in[sweep, t]
        current = current + scale * (rhs_ref[...] - applied)
    out_ref[...] = current

    for copy in p_copies + m_copies + x_copies(0) + x_copies(1):
        if copy is not p_copies[1] and copy is not p_copies[2]:
            copy.wait_send()
    for t in range(KA):
        z_wait(t)
        if t > 0:
            strip_copy(t).wait_send()
        for sweep in range(2):
            if t in MEET:
                near_copy(sweep, t).wait_send()
            elif t > 0:
                r_copy(sweep, t).wait_send()


def col_mesh(a_blocks, a_live, p_blocks, p_cols, ghost_list, policy, rates, rhs, guess):
    rows = lax.axis_size("row")
    cols = lax.axis_size("col")
    blocks = a_blocks.shape[0]
    width = rhs.shape[1]
    own_p = p_blocks.reshape(blocks, BS * KP, CB)
    vmem = pl.BlockSpec(memory_space=pltpu.VMEM)
    smem = pl.BlockSpec(memory_space=pltpu.SMEM)
    anywhere = pl.BlockSpec(memory_space=pl.ANY)
    f32, bf16 = jnp.float32, jnp.bfloat16
    dma = pltpu.SemaphoreType.DMA
    matrix, smoothed = pl.pallas_call(
        functools.partial(kernel, rows, cols),
        out_shape=(
            jax.ShapeDtypeStruct((cols, CB, rows * CB), f32),
            jax.ShapeDtypeStruct((CB, width), f32),
        ),
        in_specs=[anywhere, anywhere, vmem, vmem, smem, smem, smem, vmem, vmem, vmem],
        out_specs=(vmem, vmem),
        scratch_shapes=[
            pltpu.VMEM((KA, blocks, BS * KP, CB), f32),
            pltpu.VMEM((KA, rows, CB, rows * CB), f32),
            pltpu.VMEM((KA, rows + 1, CB, rows * CB), f32),
            pltpu.VMEM((blocks, KP * CB, 3 * BS), bf16),
            pltpu.VMEM((blocks * KP, CB, rows * CB), f32),
            pltpu.VMEM((blocks, BS, BS), f32),
            pltpu.VMEM((blocks, BS, BS), f32),
            pltpu.VMEM((2 * KA, CB), jnp.int32),
            pltpu.VMEM((cols, 2 * KA, CB), jnp.int32),
            pltpu.SMEM((cols, 2 * KA, CB), jnp.int32),
            pltpu.VMEM((2, rows, CB, width), f32),
            pltpu.VMEM((3 * rows * CB, width), bf16),
            pltpu.VMEM((2, KA, CB, width), f32),
            pltpu.VMEM((2, KA, CB, width), f32),
            pltpu.VMEM((2, KA, CB, width), f32),
            dma((2,)), dma((4,)), dma((8,)), dma((8,)), dma((cols,)), dma((cols,)),
            dma((KA, 2, rows)), dma((KA, rows + 1)), dma((KA,)), dma((KA,)),
            dma((2, rows)), dma((2, rows)), dma((2, KA)), dma((2, KA)), dma((2, KA)), dma((2, KA)),
        ],
        compiler_params=pltpu.CompilerParams(
            collective_id=0, has_side_effects=True, vmem_limit_bytes=60 * 1024 * 1024
        ),
        cost_estimate=pl.CostEstimate(
            flops=12 * KA * blocks * BS * BS * BS,
            bytes_accessed=4 * (a_blocks.size + p_blocks.size), transcendentals=0,
        ),
        name="coarse_and_sweeps",
    )(a_blocks, own_p, ghost_list, p_cols.T, p_cols.T, a_live, policy, rates, rhs, guess)
    return matrix.reshape(cols * CB, rows, 1, CB), smoothed


def on_device(a_blocks, *rest):
    blocks, slots = a_blocks.shape[:2]
    if blocks == slots == lax.axis_size("col") and lax.axis_size("row") * CB == KP * BS:
        return col_mesh(a_blocks, *rest)
    return any_mesh(a_blocks, *rest)


def solution(mesh):
    return jax.shard_map(
        on_device,
        mesh=mesh,
        in_specs=(
            P(("row", "col"), None, None, None),
            P(("row", "col"), None),
            P(("row", "col"), None, None, None),
            P(("row", "col"), None),
            P(("row", "col"), None),
            P(("row", "col")),
            P(),
            P(("row", "col"), None),
            P(("row", "col"), None),
        ),
        out_specs=(P("row", None, "col", None), P(("row", "col"), None)),
        check_vma=False,
    )
```
